32 devices in a mesh: groups: 2 (over x), slab: 8 (over z, y), cross: 2 (over core).
Axes of the slice: x: 2, y: 2, z: 4, core: 2. Of those that a mesh axis runs over, the one named last changes fastest.
Arguments:
- mode_shapes: float32 [32, 3, 4096], P(None, None, ('slab', 'cross')), may hold values from -16 to 16, as said below
- stencil: int32 [3, 8192], P(None, ('slab', 'cross')), may hold values from 0 to 255
- stencil_weight: float32 [3, 8192], P(None, ('slab', 'cross')), may hold values from 0.2 to 1
- owner_slab: int32 [8192, 1], P(('slab', 'cross')), may hold values from 0 to 7; in each aligned block of 512 rows (0 to 511, 512 to 1023, ...) at most 128 rows name the same one
- target_cell: int32 [8192], P(('slab', 'cross')), may hold values from 0 to 4095
- neighbour_codes: int32 [7, 256, 256], P(None, 'slab', 'cross'), may hold values from 0 to 9, as said below
- jacobian: bfloat16 [14, 5, 5, 256, 256], P('groups', None, None, 'slab', 'cross'), parts along dimension 0, may hold values from -1.25 to 1.25
- lift_matrix: bfloat16 [10, 3, 256, 256], P('groups', None, 'slab', 'cross'), parts along dimension 0, may hold values from -3.5 to 3.5
- pod_basis: bfloat16 [10, 256, 256, 128], P('groups', 'slab', 'cross'), parts along dimension 0, may hold values from -0.03125 to 0.03125
Outputs:
- induced: float32 [64, 5, 256, 256], P('groups', None, 'slab', 'cross'), parts along dimension 0
- reduced: float32 [64, 128], P('groups'), parts along dimension 0
The draws below stay inside these ranges and needn't reach their ends.
There are 2 independent parts, one for each index of `groups`. The reference program is written for one: setup_inputs(seed, part) draws one part's arguments, and reference() takes and returns one part's arrays. A program takes and returns all parts, laid end to end along the dimension named above; an argument that names none is the same for every part. Nothing has to cross between parts.
Inputs may be any that keep to these rules, and one draw needn't show every extreme that they name: `mode_shapes`: mode shapes whose magnitude varies over the nodes. `stencil`: entries name structural nodes of the same device's block of 256 nodes. `owner_slab`: in each aligned block of 512 rows (the rows of one device) no slab is named by more than 128 rows. `target_cell`: the owning device is the one of slab owner_slab with the surface node's own cross index. `neighbour_codes`: slot 0 holds code 4 (the cell itself); the live codes of a cell are distinct and come first, 4 or more of them; 9 marks an unused slot.
All inputs are finite; a program needn't handle non-finite values.
Results may differ from the reference program's by a relative error of at most 0.0003.
Values may be sent and summed in bfloat16 or wider, within the bound.
A program may use at most 128 MiB of HBM per device.

```python
import math
import jax
import jax.numpy as jnp
import numpy as np
from jax import lax

MODES = 32
POD = 128
NVAR = 5
NDIM = 3
STEN = 3
DEG = 7
SWEEPS = 4
CX = 32
CY = 128
SURF_DEV = 512
NS_DEV = 256
SLABS = 8
CAP = 128
NX = 256
NY = 256
NSURF = 8192
NS = 4096
N_CROSS = 2


def draw_mode_shapes(key, part):
    key = jax.random.fold_in(key, 3)
    node_pos = jnp.arange(NS, dtype=jnp.float32) / NS
    base_draw = jnp.clip(jax.random.normal(key, (MODES, NDIM, NS), jnp.float32), -5.0, 5.0)
    node_ramp = jnp.sqrt(1.0 + 2.0 * node_pos)
    return base_draw * node_ramp[None, None, :]


def draw_neighbour_codes(key, part):
    key = jax.random.fold_in(key, 7)
    key_score, key_live = jax.random.split(key)
    scores = jax.random.randint(key_score, (9, NX, NY), 0, 2 ** 20) * 16 + jnp.arange(9, dtype=jnp.int32)[:, None, None]
    scores = jnp.where((jnp.arange(9, dtype=jnp.int32) == 4)[:, None, None], -1, scores)
    ordered = jnp.argsort(scores, axis=0, stable=True)[:DEG].astype(jnp.int32)
    live_count = jax.random.randint(key_live, (1, NX, NY), 4, DEG + 1)
    slot_index = jnp.arange(DEG, dtype=jnp.int32)[:, None, None]
    return jnp.where(slot_index < live_count, ordered, 9).astype(jnp.int32)


def with_ends(array, own_key, least, largest):
    shape = array.shape
    place = [jax.random.randint(jax.random.fold_in(own_key, axis), (), 0, shape[axis]) for axis in range(len(shape))]
    array = array.at[tuple(place)].set(least)
    longest = shape.index(max(shape))
    place[longest] = (place[longest] + 1) % shape[longest]
    return array.at[tuple(place)].set(largest)


def block_levels(key, extent, pieces, least, high):
    gain, own = 1.0, jax.random.fold_in(key, 6)
    for position, blocks in pieces:
        heights = jnp.exp(jax.random.uniform(jax.random.fold_in(own, position), (blocks,), jnp.float32, least / len(pieces), high / len(pieces)))
        gain = gain * jnp.repeat(heights, extent[position] // blocks).reshape([-1 if axis == position else 1 for axis in range(len(extent))])
    return gain


def routed_block(key, own, number, rows, amount, top, bound, lean):
    order = jax.random.permutation(key, amount)
    crowded, ordinary = load_shares(amount, rows * top, bound, lean, True), load_shares(amount, rows * top, bound, lean, False)
    places = jnp.arange(amount)

    def named(sizes, turn):
        used = int((sizes > 0).sum())
        fixed = max(1, used // 4)
        passed = fixed + (places - fixed + turn * (used - fixed)) % max(1, amount - fixed)
        return jnp.zeros((amount,), jnp.int32).at[order[jnp.where(places < fixed, places, passed)]].set(jnp.asarray(sizes, jnp.int32))

    sizes = jnp.where(number % 4 == 0, named(crowded, number // 4), named(ordinary, number - number // 4 - 1))
    mixed = jax.random.permutation(jax.random.fold_in(own, 3), amount)
    donor, taker = mixed[0:amount // 2 * 2:2], mixed[1:amount // 2 * 2:2]
    room = jnp.minimum(sizes[donor] - 1, bound - sizes[taker]) // 2
    room = jnp.where((donor == order[0]) | (taker == order[0]) | (sizes[taker] == 0), 0, jnp.maximum(room, 0))
    passed = jax.random.randint(jax.random.fold_in(own, 4), (amount // 2,), 0, 1 << 20) % (room + 1)
    sizes = sizes.at[donor].add(-passed).at[taker].add(passed)
    labels = jnp.searchsorted(jnp.cumsum(sizes), jnp.arange(rows * top), side="right").astype(jnp.int32)
    grid = labels.reshape(top, rows).T
    grid = grid[jax.random.permutation(jax.random.fold_in(own, 1), rows)]
    turn = jax.random.randint(jax.random.fold_in(own, 2), (rows, 1), 0, top)
    return jnp.take_along_axis(grid, (jnp.arange(top)[None, :] + turn) % top, axis=1)


def load_shares(amount, total, limit, lean, full):
    weights = [(1 << 20) // math.isqrt(rank ** lean) + 1 for rank in range(1, amount + 1)]
    largest = limit if full else min(limit, max(-(-total // amount), total * weights[0] // sum(weights)))
    least = 1 if total - largest >= amount - 1 else 0
    counts, surplus = [largest] + [least] * (amount - 1), total - largest - least * (amount - 1)
    while surplus > 0:
        free = [i for i in range(1, amount) if counts[i] < largest] or [i for i in range(1, amount) if counts[i] < limit]
        whole, left = sum([weights[i] for i in free]), surplus
        for i in free:
            extra = min(limit - counts[i], max(1, left * weights[i] // whole), surplus)
            counts[i] = counts[i] + extra
            surplus = surplus - extra
    return np.array(counts)


def centred(key, extent, scale, limit, pieces=(), kind=jnp.bfloat16):
    entries = scale * jax.random.normal(key, extent, jnp.float32)
    if pieces:
        entries = entries * block_levels(key, extent, pieces, -0.22, 0.18)
    return jnp.clip(entries, -limit, limit).astype(kind)


def setup_inputs(seed: int = 0, part: int = 0) -> dict:
    arg_keys = jax.random.split(jax.random.key(seed), 10)
    part_keys = jax.random.split(jax.random.fold_in(arg_keys[9], part), 10)
    mode_shapes = draw_mode_shapes(jax.random.fold_in(arg_keys[9], 71), part)
    stencil = with_ends(jax.random.randint(arg_keys[1], (STEN, NSURF), 0, NS_DEV), jax.random.fold_in(arg_keys[1], 1), 0, NS_DEV - 1).astype(jnp.int32)
    stencil_weight = jnp.clip(0.2 + 0.8 * jax.random.uniform(arg_keys[2], (STEN, NSURF), jnp.float32) ** block_levels(arg_keys[2], (STEN, NSURF), ((1, 16),), -0.2, 0.2), 0.2, 1.0)
    owner_slab_keys = jax.random.split(jax.random.fold_in(arg_keys[3], 1), NSURF // SURF_DEV)
    owner_slab_turns = jax.random.permutation(jax.random.fold_in(arg_keys[3], 3), NSURF // SURF_DEV)
    owner_slab = jax.vmap(lambda own, number: routed_block(jax.random.fold_in(arg_keys[3], 2), own, number, SURF_DEV, SLABS, 1, CAP, 2))(owner_slab_keys, owner_slab_turns).reshape((NSURF, 1))
    target_cell = with_ends(jax.random.randint(arg_keys[4], (NSURF,), 0, CX * CY), jax.random.fold_in(arg_keys[4], 1), 0, (CX * CY) - 1).astype(jnp.int32)
    neighbour_codes = draw_neighbour_codes(jax.random.fold_in(arg_keys[9], 71), part)
    jacobian = centred(part_keys[6], (DEG, NVAR, NVAR, NX, NY), (NVAR * 5) ** -0.5, 1.25, ((3, 8), (4, 2)))
    lift_matrix = centred(part_keys[7], (NVAR, NDIM, NX, NY), NDIM ** -0.5, 3.5, ((2, 8), (3, 2)))
    pod_basis = centred(part_keys[8], (NVAR, NX, NY, POD), (NVAR * NX * NY // 8) ** -0.5, 0.03125, ((1, 8), (2, 2)))
    return dict(mode_shapes=mode_shapes, stencil=stencil, stencil_weight=stencil_weight, owner_slab=owner_slab, target_cell=target_cell, neighbour_codes=neighbour_codes, jacobian=jacobian, lift_matrix=lift_matrix, pod_basis=pod_basis)


SPREAD = 0.24

def lift_state(lift_gain, field_now):
    accumulated = 0.0
    for component in range(lift_gain.shape[1]):
        accumulated = accumulated + lift_gain[:, component] * jnp.expand_dims(field_now[..., component, :, :], -3)
    return accumulated

def offset_blocks(codes, jacobian):
    zero_block = jnp.zeros((), jnp.bfloat16)
    stacked = []
    for offset_code in range(9):
        chosen = jnp.where((codes == offset_code)[:, None, None], jacobian, zero_block)
        stacked.append(lax.optimization_barrier(jnp.sum(chosen, axis=0, dtype=jnp.float32)))
    return jnp.stack(stacked)

def apply_blocks(blocks, padded, cell_rows, cell_cols):
    accumulated = 0.0
    for offset_code in range(9):
        start_x = offset_code // 3
        start_y = offset_code % 3
        shifted = padded[..., start_x:start_x + cell_rows, start_y:start_y + cell_cols]
        for component in range(blocks.shape[2]):
            accumulated = accumulated + blocks[offset_code, :, component] * jnp.expand_dims(shifted[..., component, :, :], -3)
    return accumulated

def reference(mode_shapes, stencil, stencil_weight, owner_slab, target_cell, neighbour_codes, jacobian, lift_matrix, pod_basis):
    squares = lax.optimization_barrier(jnp.sum(mode_shapes * mode_shapes, axis=(1, 2)))
    scale_rms = jnp.sqrt(squares / (NDIM * NS) + 1e-06)
    normed = mode_shapes / scale_rms[:, None, None]
    source = jnp.arange(NSURF, dtype=jnp.int32) // SURF_DEV
    node_index = source[None, :] * NS_DEV + stencil
    picked = normed[:, :, node_index]
    surface = lax.optimization_barrier(jnp.sum(stencil_weight[None, None] * picked, axis=2))
    cross_index = source % N_CROSS
    row_index = owner_slab[:, 0] * CX + target_cell // CY
    col_index = cross_index * CY + target_cell % CY
    flat_cell = row_index * NY + col_index
    deposit = jnp.zeros((MODES, NDIM, NX * NY), jnp.float32).at[:, :, flat_cell].add(surface)
    deposit = deposit.reshape(MODES, NDIM, NX, NY)
    blocks = offset_blocks(neighbour_codes, jacobian)
    lift_gain = lift_matrix.astype(jnp.float32)

    def extend_mode(source_field):
        field_now = source_field
        for sweep_index in range(SWEEPS):
            padded = jnp.pad(field_now, ((0, 0), (1, 1), (1, 1)))
            field_now = source_field + SPREAD * (padded[:, 2:, 1:-1] + padded[:, :-2, 1:-1] + padded[:, 1:-1, 2:] + padded[:, 1:-1, :-2])
        state = lift_state(lift_gain, field_now)
        padded = jnp.pad(state, ((0, 0), (1, 1), (1, 1)))
        return apply_blocks(blocks, padded, NX, NY)
    induced = lax.map(extend_mode, deposit)
    reduced = jnp.dot(induced.reshape(MODES, -1), pod_basis.reshape(-1, POD).astype(jnp.float32), precision=lax.Precision.HIGHEST, preferred_element_type=jnp.float32)
    return (induced, reduced)
```

```python
import functools

import jax
import jax.numpy as jnp
from jax import lax
from jax.experimental import pallas as pl
from jax.experimental.pallas import tpu as pltpu
from jax.sharding import PartitionSpec as P

SWEEPS = 4


SPREAD = 0.24

RIM = SWEEPS + 1

LANES = 128

MESH = pl.DeviceIdType.MESH

NT = (((1,), (1,)), ((), ()))


def split_2(value):
    high = value.astype(jnp.bfloat16)
    low = (value - high.astype(jnp.float32)).astype(jnp.bfloat16)
    return high, low


def route_kernel(
    slabs,
    rows,
    modes_dim,
    comps,
    node_total,
    modes_ref,
    stencil_ref,
    weight_ref,
    owner_ref,
    target_ref,
    lift_ref,
    field_ref,
    scale_ref,
    send_buf,
    recv_buf,
    arrived,
    labels,
    squares,
    send_sem,
    recv_sem,
    edge_send,
    edge_recv,
    pair_send,
    pair_recv,
    sq_send,
    sq_recv,
):
    me = lax.axis_index("slab")
    mine = lax.axis_index("cross")
    other = 1 - mine
    nodes = modes_ref.shape[1]
    surf = stencil_ref.shape[1]
    data = modes_dim * comps

    barrier = pltpu.get_barrier_semaphore()
    for k in range(1, slabs):
        pl.semaphore_signal(
            barrier, inc=1, device_id={"slab": lax.rem(me + k, slabs)}, device_id_type=MESH
        )
    pl.semaphore_signal(barrier, inc=1, device_id={"cross": other}, device_id_type=MESH)

    node_id = lax.broadcasted_iota(jnp.int32, (nodes, surf), 0)
    mix = jnp.zeros((nodes, surf), jnp.float32)
    for j in range(stencil_ref.shape[0]):
        mix = mix + jnp.where(stencil_ref[j : j + 1, :] == node_id, weight_ref[j : j + 1, :], 0.0)
    surface = jnp.dot(
        modes_ref[...], mix, precision=lax.Precision.HIGHEST, preferred_element_type=jnp.float32
    )
    owner = owner_ref[...]
    slab_id = lax.broadcasted_iota(jnp.int32, (slabs, surf), 0)
    named = (owner == slab_id).astype(jnp.float32)
    before = (
        lax.broadcasted_iota(jnp.int32, (surf, surf), 0)
        < lax.broadcasted_iota(jnp.int32, (surf, surf), 1)
    ).astype(jnp.bfloat16)
    ahead = jnp.dot(named.astype(jnp.bfloat16), before, preferred_element_type=jnp.float32)
    rank = jnp.sum(ahead * named, axis=0, keepdims=True).astype(jnp.int32)
    position = owner * LANES + rank
    target = target_ref[...]
    target_low = lax.rem(target, 64)
    row_id = lax.broadcasted_iota(jnp.int32, surface.shape, 0)
    high = surface.astype(jnp.bfloat16).astype(jnp.float32)
    low = surface - high
    high = jnp.where(row_id == data, (target - target_low).astype(jnp.float32), high)
    high = jnp.where(row_id == data + 1, 1.0, high)
    low = jnp.where(row_id == data, target_low.astype(jnp.float32), low)
    both = jnp.concatenate([high, low], axis=0).astype(jnp.bfloat16)
    modes = modes_ref[...]
    square_row = lax.dot_general(
        jnp.ones((8, nodes), jnp.float32),
        modes * modes,
        NT,
        precision=lax.Precision.HIGHEST,
        preferred_element_type=jnp.float32,
    )[0:1]
    slot_id = lax.broadcasted_iota(jnp.int32, (LANES, surf), 0)
    out_rows = send_buf.shape[1]
    out_id = lax.broadcasted_iota(jnp.int32, (out_rows, LANES), 0)

    pl.semaphore_wait(barrier, slabs)
    copies = []
    for step in range(slabs):
        k = (step + 1) % slabs
        dest = lax.rem(me + k, slabs)
        onehot = (position == slot_id + dest * LANES).astype(jnp.float32).astype(jnp.bfloat16)
        packed = lax.dot_general(both, onehot, NT, preferred_element_type=jnp.float32)
        block = packed[0:out_rows] + packed[LANES : LANES + out_rows]
        empty = 1.0 - block[data + 1 : data + 2]
        block = jnp.where(out_id == data, block - 65536.0 * empty, block)
        block = jnp.where(out_id == data + 2, square_row, block)
        if k == 0:
            recv_buf[0] = block
        else:
            send_buf[k] = block
            copy = pltpu.make_async_remote_copy(
                src_ref=send_buf.at[k],
                dst_ref=recv_buf.at[k],
                send_sem=send_sem.at[k],
                recv_sem=recv_sem.at[k],
                device_id={"slab": dest},
                device_id_type=MESH,
            )
            copy.start()
            copies.append(copy)

    field_ref[mine, RIM : RIM + rows, data:, :] = lift_ref[...]

    @pl.when(me == 0)
    def _():
        field_ref[mine, 0:RIM] = jnp.zeros((RIM,) + field_ref.shape[2:], jnp.float32)

    @pl.when(me == slabs - 1)
    def _():
        field_ref[mine, RIM + rows :] = jnp.zeros((RIM,) + field_ref.shape[2:], jnp.float32)

    total = square_row
    for k in range(slabs):
        if k > 0:
            copies[k - 1].wait_recv()
            total = total + recv_buf[k, data + 2 : data + 3]
        head, tail = split_2(recv_buf[k, 0:data])
        arrived[0:data, k * LANES : (k + 1) * LANES] = head
        arrived[data:, k * LANES : (k + 1) * LANES] = tail
        labels[0:1, k * LANES : (k + 1) * LANES] = recv_buf[k, data : data + 1].astype(jnp.int32)

    squares[0] = jnp.broadcast_to(total, (8, LANES))
    sq_copy = pltpu.make_async_remote_copy(
        src_ref=squares.at[0],
        dst_ref=squares.at[1],
        send_sem=sq_send,
        recv_sem=sq_recv,
        device_id={"cross": other},
        device_id_type=MESH,
    )
    sq_copy.start()

    cell_id = lax.broadcasted_iota(jnp.int32, (2 * LANES, slabs * LANES), 0)
    pairs = rows // 2

    def deposit(i, carry):
        pair = lax.rem(i + pairs - 3, pairs)
        hit = (labels[0:1, :] == cell_id + pair * (2 * LANES)).astype(jnp.float32)
        got = lax.dot_general(
            arrived[...], hit.astype(jnp.bfloat16), NT, preferred_element_type=jnp.float32
        )
        got = got[0:data] + got[data:]
        field_ref[mine, RIM + 2 * pair, 0:data, :] = got[:, 0:LANES]
        field_ref[mine, RIM + 2 * pair + 1, 0:data, :] = got[:, LANES:]
        return carry

    up = pltpu.make_async_remote_copy(
        src_ref=field_ref.at[mine, pl.ds(rows, RIM)],
        dst_ref=field_ref.at[mine, pl.ds(0, RIM)],
        send_sem=edge_send.at[0],
        recv_sem=edge_recv.at[0],
        device_id={"slab": lax.rem(me + 1, slabs)},
        device_id_type=MESH,
    )
    down = pltpu.make_async_remote_copy(
        src_ref=field_ref.at[mine, pl.ds(RIM, RIM)],
        dst_ref=field_ref.at[mine, pl.ds(RIM + rows, RIM)],
        send_sem=edge_send.at[1],
        recv_sem=edge_recv.at[1],
        device_id={"slab": lax.rem(me + slabs - 1, slabs)},
        device_id_type=MESH,
    )

    def across(n, start, size):
        return pltpu.make_async_remote_copy(
            src_ref=field_ref.at[mine, pl.ds(start, size)],
            dst_ref=field_ref.at[mine, pl.ds(start, size)],
            send_sem=pair_send.at[n],
            recv_sem=pair_recv.at[n],
            device_id={"cross": other},
            device_id_type=MESH,
        )

    middle = across(0, RIM, rows)
    low_rim = across(1, 0, RIM)
    high_rim = across(2, RIM + rows, RIM)

    lax.fori_loop(0, 3, deposit, 0)

    @pl.when(me < slabs - 1)
    def _():
        up.start()

    lax.fori_loop(3, 6, deposit, 0)

    @pl.when(me > 0)
    def _():
        down.start()

    lax.fori_loop(6, pairs, deposit, 0)
    middle.start()

    @pl.when(me > 0)
    def _():
        up.wait_recv()

    low_rim.start()

    @pl.when(me < slabs - 1)
    def _():
        down.wait_recv()

    high_rim.start()

    sq_copy.wait()
    whole = squares[0, 0:1] + squares[1, 0:1]
    lane = lax.broadcasted_iota(jnp.int32, (modes_dim, LANES), 1)
    mode = lax.broadcasted_iota(jnp.int32, (modes_dim, LANES), 0)
    per_mode = jnp.sum(
        jnp.where((lax.rem(lane, modes_dim) == mode) & (lane < data), whole, 0.0),
        axis=1,
        keepdims=True,
    )
    inverse = 1.0 / jnp.sqrt(per_mode / node_total + 1e-06)
    scale_ref[...] = jnp.broadcast_to(inverse, scale_ref.shape)

    for copy in copies:
        copy.wait_send()

    @pl.when(me < slabs - 1)
    def _():
        up.wait_send()

    @pl.when(me > 0)
    def _():
        down.wait_send()

    middle.wait()
    low_rim.wait()
    high_rim.wait()


def local_kernel(
    slabs,
    rows,
    modes_dim,
    comps,
    variables,
    field_ref,
    scale_ref,
    codes_ref,
    jac_ref,
    pod_ref,
    induced_ref,
    partial_ref,
    ping,
    pong,
    state,
    blocks,
):
    me = lax.axis_index("slab")
    mine = lax.axis_index("cross")
    other = 1 - mine
    data = modes_dim * comps
    planes = rows + 2 * RIM
    lane = lax.broadcasted_iota(jnp.int32, (modes_dim, LANES), 1)
    first, last = lane == 0, lane == LANES - 1
    square = variables * variables

    def select(pair, carry):
        for x0 in range(0, rows, 8):
            chosen = [jac_ref[k, pair, x0 : x0 + 8, :].astype(jnp.float32) for k in range(7)]
            codes = [codes_ref[k, x0 : x0 + 8, :] for k in range(7)]
            for code in range(9):
                value = jnp.zeros((8, LANES), jnp.float32)
                for k in range(7):
                    value = jnp.where(codes[k] == code, chosen[k], value)
                blocks[code * square + pair, x0 : x0 + 8, :] = value
        return carry

    lax.fori_loop(0, square, select, 0)

    def sweep(source, result, edge):
        def plane(x, carry):
            at = x - RIM + me * rows
            inside = ((at >= 0) & (at < slabs * rows)).astype(jnp.float32)
            for comp in range(comps):
                part = pl.ds(comp * modes_dim, modes_dim)
                left, right = source[0, x, part, :], source[1, x, part, :]
                left_up, right_up = pltpu.roll(left, 1, 1), pltpu.roll(right, 1, 1)
                left_down = pltpu.roll(left, LANES - 1, 1)
                right_down = pltpu.roll(right, LANES - 1, 1)
                near_left = jnp.where(first, 0.0, left_up) + jnp.where(last, right_down, left_down)
                near_right = jnp.where(first, left_up, right_up) + jnp.where(last, 0.0, right_down)
                for tile, near in ((0, near_left), (1, near_right)):
                    near = near + source[tile, x - 1, part, :] + source[tile, x + 1, part, :]
                    result[tile, x, part, :] = (
                        field_ref[tile, x, part, :] + SPREAD * near
                    ) * inside
            return carry

        lax.fori_loop(edge, planes - edge, plane, 0)

    sweep(field_ref, ping, 1)
    sweep(ping, pong, 2)
    sweep(pong, ping, 3)
    sweep(ping, pong, 4)

    here = (mine == 0).astype(jnp.float32)
    there = 1.0 - here

    def lift(x, carry):
        for b in range(variables):
            own = jnp.zeros((modes_dim, LANES), jnp.float32)
            far = jnp.zeros((modes_dim, LANES), jnp.float32)
            for comp in range(comps):
                part = pl.ds(comp * modes_dim, modes_dim)
                row = pl.ds(data + comp * variables + b, 1)
                own = own + field_ref[mine, x + RIM - 1, row, :] * pong[mine, x + RIM - 1, part, :]
                far = (
                    far + field_ref[other, x + RIM - 1, row, :] * pong[other, x + RIM - 1, part, :]
                )
            state[1, x, b] = own
            state[0, x, b] = jnp.where(first, pltpu.roll(far, 1, 1) * there, pltpu.roll(own, 1, 1))
            state[2, x, b] = jnp.where(
                last, pltpu.roll(far, LANES - 1, 1) * here, pltpu.roll(own, LANES - 1, 1)
            )
        return carry

    lax.fori_loop(0, rows + 2, lift, 0)

    stride = variables * rows

    def apply(x, total):
        sums = [jnp.zeros((modes_dim, LANES), jnp.float32) for _ in range(variables)]
        for code in range(9):
            for a in range(variables):
                value = state[code % 3, x + code // 3, a]
                for b in range(variables):
                    gain = blocks[code * square + b * variables + a, pl.ds(x, 1), :]
                    sums[b] = sums[b] + gain * value
        for b in range(variables):
            result = sums[b] * scale_ref[...]
            induced_ref[pl.ds(b * rows + x, modes_dim, stride=stride), :] = result
            high, low = split_2(result)
            total = total + jnp.dot(
                jnp.concatenate([high, low], axis=0),
                pod_ref[b, x],
                preferred_element_type=jnp.float32,
            )
        return total

    total = lax.fori_loop(
        0, rows, apply, jnp.zeros((2 * modes_dim, partial_ref.shape[1]), jnp.float32)
    )
    partial_ref[...] = total[0:modes_dim] + total[modes_dim:]


def sum_kernel(
    slabs, crosses, part_ref, out_ref, got, mine_sum, send_sem, recv_sem, back_send, back_recv
):
    me = lax.axis_index("slab") * crosses + lax.axis_index("cross")
    count = slabs * crosses

    def peer(k):
        at = lax.rem(me + k, count)
        return at, {"slab": lax.div(at, crosses), "cross": lax.rem(at, crosses)}

    barrier = pltpu.get_barrier_semaphore()
    for k in range(1, count):
        pl.semaphore_signal(barrier, inc=1, device_id=peer(k)[1], device_id_type=MESH)
    pl.semaphore_wait(barrier, count - 1)
    copies = []
    for k in range(1, count):
        at, device = peer(k)
        copy = pltpu.make_async_remote_copy(
            src_ref=part_ref.at[at],
            dst_ref=got.at[k],
            send_sem=send_sem.at[k],
            recv_sem=recv_sem.at[k],
            device_id=device,
            device_id_type=MESH,
        )
        copy.start()
        copies.append(copy)
    total = part_ref[me]
    for k in range(1, count):
        copies[k - 1].wait_recv()
        total = total + got[k]
    mine_sum[...] = total
    out_ref[me] = total
    backs = []
    for k in range(1, count):
        at, device = peer(k)
        copy = pltpu.make_async_remote_copy(
            src_ref=mine_sum,
            dst_ref=out_ref.at[me],
            send_sem=back_send.at[k],
            recv_sem=back_recv.at[k],
            device_id=device,
            device_id_type=MESH,
        )
        copy.start()
        backs.append(copy)
    for copy in copies:
        copy.wait_send()
    for copy in backs:
        copy.wait()


VMEM = pl.BlockSpec(memory_space=pltpu.VMEM)


def fast_body(
    mode_shapes,
    stencil,
    stencil_weight,
    owner_slab,
    target_cell,
    neighbour_codes,
    jacobian,
    lift_matrix,
    pod_basis,
):
    slabs = lax.axis_size("slab")
    crosses = lax.axis_size("cross")
    modes_dim, comps, nodes = mode_shapes.shape
    surf = owner_slab.shape[0]
    rows, cols = neighbour_codes.shape[1:]
    variables = lift_matrix.shape[0]
    pod = pod_basis.shape[-1]
    data = modes_dim * comps
    lift_rows = 16
    planes = rows + 2 * RIM
    count = slabs * crosses
    modes = jnp.pad(
        mode_shapes.transpose(1, 0, 2).reshape(data, nodes), ((0, LANES - data), (0, 0))
    )
    lift = jnp.pad(
        lift_matrix.transpose(2, 1, 0, 3).reshape(rows, comps * variables, cols),
        ((0, 0), (0, lift_rows - comps * variables), (0, 0)),
    ).astype(jnp.float32)
    dma = pltpu.SemaphoreType.DMA
    field, scale = pl.pallas_call(
        functools.partial(
            route_kernel, slabs, rows, modes_dim, comps, float(comps * nodes * count)
        ),
        out_shape=(
            jax.ShapeDtypeStruct((crosses, planes, data + lift_rows, cols), jnp.float32),
            jax.ShapeDtypeStruct((modes_dim, LANES), jnp.float32),
        ),
        in_specs=[VMEM] * 6,
        out_specs=(VMEM, VMEM),
        scratch_shapes=[
            pltpu.VMEM((slabs, data + 8, LANES), jnp.float32),
            pltpu.VMEM((slabs, data + 8, LANES), jnp.float32),
            pltpu.VMEM((2 * data, slabs * LANES), jnp.bfloat16),
            pltpu.VMEM((8, slabs * LANES), jnp.int32),
            pltpu.VMEM((2, 8, LANES), jnp.float32),
            dma((slabs,)),
            dma((slabs,)),
            dma((2,)),
            dma((2,)),
            dma((3,)),
            dma((3,)),
            dma,
            dma,
        ],
        compiler_params=pltpu.CompilerParams(
            collective_id=0, has_side_effects=True, vmem_limit_bytes=40 * 1024 * 1024
        ),
    )(
        modes,
        stencil,
        stencil_weight,
        owner_slab.reshape(1, surf),
        target_cell.reshape(1, surf),
        lift,
    )
    scratch = pltpu.VMEM((crosses, planes, data, cols), jnp.float32)
    induced, partial_value = pl.pallas_call(
        functools.partial(local_kernel, slabs, rows, modes_dim, comps, variables),
        out_shape=(
            jax.ShapeDtypeStruct((modes_dim * variables * rows, cols), jnp.float32),
            jax.ShapeDtypeStruct((modes_dim, pod), jnp.float32),
        ),
        in_specs=[VMEM] * 5,
        out_specs=(VMEM, VMEM),
        scratch_shapes=[
            scratch,
            scratch,
            pltpu.VMEM((3, rows + 2, variables, modes_dim, cols), jnp.float32),
            pltpu.VMEM((9 * variables * variables, rows, cols), jnp.float32),
        ],
        compiler_params=pltpu.CompilerParams(vmem_limit_bytes=52 * 1024 * 1024),
    )(
        field,
        scale,
        neighbour_codes,
        jacobian.reshape(jacobian.shape[0], variables * variables, rows, cols),
        pod_basis,
    )
    share = modes_dim // count
    reduced = pl.pallas_call(
        functools.partial(sum_kernel, slabs, crosses),
        out_shape=jax.ShapeDtypeStruct((count, share, pod), jnp.float32),
        in_specs=[VMEM],
        out_specs=VMEM,
        scratch_shapes=[
            pltpu.VMEM((count, share, pod), jnp.float32),
            pltpu.VMEM((share, pod), jnp.float32),
            dma((count,)),
            dma((count,)),
            dma((count,)),
            dma((count,)),
        ],
        compiler_params=pltpu.CompilerParams(collective_id=1, has_side_effects=True),
    )(partial_value.reshape(count, share, pod))
    return (
        induced.reshape(modes_dim, variables, rows, cols),
        reduced.reshape(modes_dim, pod),
    )


def padded_2(block, sides, width):
    for axis, dim in sides:
        count = lax.axis_size(axis)
        forward = [(i, i + 1) for i in range(count - 1)]
        backward = [(target, source) for source, target in forward]
        low = lax.ppermute(
            lax.slice_in_dim(block, block.shape[dim] - width, None, axis=dim), axis, forward
        )
        high = lax.ppermute(lax.slice_in_dim(block, 0, width, axis=dim), axis, backward)
        block = jnp.concatenate([low, block, high], axis=dim)
    return block


def lift_state(lift_gain, field_now):
    accumulated = 0.0
    for component in range(lift_gain.shape[1]):
        accumulated = accumulated + lift_gain[:, component] * jnp.expand_dims(
            field_now[..., component, :, :], -3
        )
    return accumulated


def offset_blocks(codes, jacobian):
    zero_block = jnp.zeros((), jnp.bfloat16)
    stacked = []
    for offset_code in range(9):
        chosen = jnp.where((codes == offset_code)[:, None, None], jacobian, zero_block)
        stacked.append(jnp.sum(chosen, axis=0, dtype=jnp.float32))
    return jnp.stack(stacked)


def apply_blocks(blocks, padded, cell_rows, cell_cols):
    accumulated = 0.0
    for offset_code in range(9):
        start_x = offset_code // 3
        start_y = offset_code % 3
        shifted = padded[..., start_x : start_x + cell_rows, start_y : start_y + cell_cols]
        for component in range(blocks.shape[2]):
            accumulated = accumulated + blocks[offset_code, :, component] * jnp.expand_dims(
                shifted[..., component, :, :], -3
            )
    return accumulated


def body(
    mode_shapes,
    stencil,
    stencil_weight,
    owner_slab,
    target_cell,
    neighbour_codes,
    jacobian,
    lift_matrix,
    pod_basis,
):
    slab_count = lax.axis_size("slab")
    cross_count = lax.axis_size("cross")
    mode_count, space_dims, nodes_dev = mode_shapes.shape
    surf_dev = owner_slab.shape[0]
    capacity = 2 * surf_dev // slab_count
    cell_rows = neighbour_codes.shape[1]
    cell_cols = neighbour_codes.shape[2]
    total_nodes = nodes_dev * slab_count * cross_count
    squares = jnp.sum(mode_shapes * mode_shapes, axis=(1, 2))
    scale_rms = jnp.sqrt(lax.psum(squares, ("slab", "cross")) / (space_dims * total_nodes) + 1e-06)
    shapes_used = mode_shapes / scale_rms[:, None, None]
    picked = shapes_used[:, :, stencil]
    surface = jnp.sum(stencil_weight[None, None] * picked, axis=2)
    dest_slab = owner_slab[:, 0]
    onehot = (dest_slab[:, None] == jnp.arange(slab_count, dtype=jnp.int32)[None, :]).astype(
        jnp.int32
    )
    slot_rank = jnp.sum((jnp.cumsum(onehot, axis=0) - 1) * onehot, axis=1)
    position = dest_slab * capacity + slot_rank
    payload = jnp.zeros((mode_count * space_dims, slab_count * capacity), jnp.float32)
    payload = payload.at[:, position].set(surface.reshape(mode_count * space_dims, surf_dev))
    labels = jnp.zeros((1, slab_count * capacity), jnp.int32).at[0, position].set(target_cell)
    arrived, arrived_cells = (
        lax.all_to_all(payload, "slab", split_axis=1, concat_axis=1, tiled=True),
        lax.all_to_all(labels, "slab", split_axis=1, concat_axis=1, tiled=True),
    )
    deposit = jnp.zeros((mode_count * space_dims, cell_rows * cell_cols), jnp.float32)
    deposit = (
        deposit.at[:, arrived_cells[0]]
        .add(arrived)
        .reshape(mode_count, space_dims, cell_rows, cell_cols)
    )
    rim_width = SWEEPS + 1
    source_padded = padded_2(deposit, (("slab", 2), ("cross", 3)), rim_width)
    grid_x = (
        lax.axis_index("slab") * cell_rows
        - rim_width
        + jnp.arange(cell_rows + 2 * rim_width, dtype=jnp.int32)
    )
    grid_y = (
        lax.axis_index("cross") * cell_cols
        - rim_width
        + jnp.arange(cell_cols + 2 * rim_width, dtype=jnp.int32)
    )
    inside_x = (grid_x >= 0) & (grid_x < cell_rows * slab_count)
    inside_y = (grid_y >= 0) & (grid_y < cell_cols * cross_count)
    inside_mask = (inside_x[:, None] & inside_y[None, :]).astype(jnp.float32)
    field_now = source_padded
    for sweep_index in range(SWEEPS):
        edge_start = sweep_index + 1
        upper_x = cell_rows + 2 * rim_width - edge_start
        upper_y = cell_cols + 2 * rim_width - edge_start
        neighbours = (
            field_now[..., 2:, 1:-1]
            + field_now[..., :-2, 1:-1]
            + field_now[..., 1:-1, 2:]
            + field_now[..., 1:-1, :-2]
        )
        field_now = (
            source_padded[..., edge_start:upper_x, edge_start:upper_y] + SPREAD * neighbours
        ) * inside_mask[edge_start:upper_x, edge_start:upper_y]
    lift_padded = padded_2(lift_matrix, (("slab", 2), ("cross", 3)), 1)
    state_padded = lift_state(lift_padded.astype(jnp.float32), field_now)
    blocks = offset_blocks(neighbour_codes, jacobian)
    induced = apply_blocks(blocks, state_padded, cell_rows, cell_cols)
    partial_value = jnp.dot(
        induced.reshape(mode_count, -1),
        pod_basis.reshape(-1, pod_basis.shape[-1]),
        precision=lax.Precision.HIGHEST,
        preferred_element_type=jnp.float32,
    )
    reduced = lax.psum(partial_value, ("slab", "cross"))
    return (induced, reduced)


def solution(mesh):
    in_specs = (
        P(None, None, ("slab", "cross")),
        P(None, ("slab", "cross")),
        P(None, ("slab", "cross")),
        P(("slab", "cross"), None),
        P(("slab", "cross")),
        P(None, "slab", "cross"),
        P("groups", None, None, "slab", "cross"),
        P("groups", None, "slab", "cross"),
        P("groups", "slab", "cross", None),
    )
    out_specs = (P("groups", None, "slab", "cross"), P("groups", None))
    slabs, crosses = mesh.shape["slab"], mesh.shape["cross"]
    chosen = fast_body if crosses == 2 and slabs == 8 else body
    return jax.shard_map(chosen, mesh=mesh, in_specs=in_specs, out_specs=out_specs, check_vma=False)
```

```python
import functools

import jax
import jax.numpy as jnp
from jax import lax
from jax.experimental import pallas as pl
from jax.experimental.pallas import tpu as pltpu
from jax.sharding import PartitionSpec as P

SWEEPS = 4


SPREAD = 0.24

RIM = SWEEPS + 1

LANES = 128

MESH = pl.DeviceIdType.MESH

NT = (((1,), (1,)), ((), ()))


def split_2(value):
    high = value.astype(jnp.bfloat16)
    low = (value - high.astype(jnp.float32)).astype(jnp.bfloat16)
    return high, low


def whole_kernel(
    slabs,
    rows,
    modes_dim,
    comps,
    variables,
    node_total,
    shapes_hbm,
    stencil_hbm,
    weight_hbm,
    owner_hbm,
    target_hbm,
    lift_hbm,
    codes_hbm,
    jac_hbm,
    pod_hbm,
    induced_hbm,
    reduced_ref,
    stencil_ref,
    weight_ref,
    owner_ref,
    target_ref,
    lift_ref,
    codes_ref,
    jac_ref,
    pod_ref,
    modes_ref,
    field_ref,
    scale_ref,
    send_buf,
    recv_buf,
    arrived,
    labels,
    squares,
    ping,
    pong,
    state,
    blocks,
    pending,
    induced_ref,
    part_ref,
    got,
    mine_sum,
    sum_ref,
    fetch_sem,
    out_sem,
    send_sem,
    recv_sem,
    edge_send,
    edge_recv,
    pair_send,
    pair_recv,
    sq_send,
    sq_recv,
    part_send,
    part_recv,
    back_send,
    back_recv,
):
    me = lax.axis_index("slab")
    mine = lax.axis_index("cross")
    other = 1 - mine
    nodes = modes_ref.shape[1]
    count = 2 * slabs
    data = modes_dim * comps
    rank_here = me * 2 + mine
    surf = stencil_ref.shape[1]

    fetched = [
        pltpu.make_async_copy(source, held, fetch_sem.at[n])
        for n, (source, held) in enumerate(
            (
                (shapes_hbm, modes_ref.at[pl.ds(0, data)]),
                (stencil_hbm, stencil_ref),
                (weight_hbm, weight_ref),
                (owner_hbm, owner_ref),
                (target_hbm, target_ref),
                (lift_hbm, lift_ref),
                (codes_hbm, codes_ref),
                (jac_hbm, jac_ref),
                (pod_hbm, pod_ref),
            )
        )
    ]
    for copy in fetched:
        copy.start()

    def peer(k):
        at = lax.rem(rank_here + k, count)
        return at, {"slab": lax.div(at, 2), "cross": lax.rem(at, 2)}

    barrier = pltpu.get_barrier_semaphore()
    for k in range(1, count):
        pl.semaphore_signal(barrier, inc=1, device_id=peer(k)[1], device_id_type=MESH)

    for copy in fetched[0:6]:
        copy.wait()
    modes_ref[data:, :] = jnp.zeros((LANES - data, nodes), jnp.float32)

    node_id = lax.broadcasted_iota(jnp.int32, (nodes, surf), 0)
    mix = jnp.zeros((nodes, surf), jnp.float32)
    for j in range(stencil_ref.shape[0]):
        mix = mix + jnp.where(stencil_ref[j : j + 1, :] == node_id, weight_ref[j : j + 1, :], 0.0)
    surface = jnp.dot(
        modes_ref[...], mix, precision=lax.Precision.HIGHEST, preferred_element_type=jnp.float32
    )
    owner = owner_ref[...]
    slab_id = lax.broadcasted_iota(jnp.int32, (slabs, surf), 0)
    named = (owner == slab_id).astype(jnp.float32)
    before = (
        lax.broadcasted_iota(jnp.int32, (surf, surf), 0)
        < lax.broadcasted_iota(jnp.int32, (surf, surf), 1)
    ).astype(jnp.bfloat16)
    ahead = jnp.dot(named.astype(jnp.bfloat16), before, preferred_element_type=jnp.float32)
    rank = jnp.sum(ahead * named, axis=0, keepdims=True).astype(jnp.int32)
    position = owner * LANES + rank
    target = target_ref[...]
    target_low = lax.rem(target, 64)
    row_id = lax.broadcasted_iota(jnp.int32, surface.shape, 0)
    high = surface.astype(jnp.bfloat16).astype(jnp.float32)
    low = surface - high
    high = jnp.where(row_id == data, (target - target_low).astype(jnp.float32), high)
    high = jnp.where(row_id == data + 1, 1.0, high)
    low = jnp.where(row_id == data, target_low.astype(jnp.float32), low)
    both = jnp.concatenate([high, low], axis=0).astype(jnp.bfloat16)
    modes = modes_ref[...]
    square_row = lax.dot_general(
        jnp.ones((8, nodes), jnp.float32),
        modes * modes,
        NT,
        precision=lax.Precision.HIGHEST,
        preferred_element_type=jnp.float32,
    )[0:1]
    slot_id = lax.broadcasted_iota(jnp.int32, (LANES, surf), 0)
    out_rows = send_buf.shape[1]
    out_id = lax.broadcasted_iota(jnp.int32, (out_rows, LANES), 0)

    pl.semaphore_wait(barrier, count - 1)
    copies = []
    for step in range(slabs):
        k = (step + 1) % slabs
        dest = lax.rem(me + k, slabs)
        onehot = (position == slot_id + dest * LANES).astype(jnp.float32).astype(jnp.bfloat16)
        packed = lax.dot_general(both, onehot, NT, preferred_element_type=jnp.float32)
        block = packed[0:out_rows] + packed[LANES : LANES + out_rows]
        empty = 1.0 - block[data + 1 : data + 2]
        block = jnp.where(out_id == data, block - 65536.0 * empty, block)
        block = jnp.where(out_id == data + 2, square_row, block)
        if k == 0:
            recv_buf[0] = block
        else:
            send_buf[k] = block
            copy = pltpu.make_async_remote_copy(
                src_ref=send_buf.at[k],
                dst_ref=recv_buf.at[k],
                send_sem=send_sem.at[k],
                recv_sem=recv_sem.at[k],
                device_id={"slab": dest},
                device_id_type=MESH,
            )
            copy.start()
            copies.append(copy)

    for comp in range(comps):
        for b in range(variables):
            field_ref[mine, RIM : RIM + rows, data + comp * variables + b, :] = lift_ref[
                b, comp
            ].astype(jnp.float32)
    field_ref[mine, RIM : RIM + rows, data + comps * variables, :] = jnp.zeros(
        (rows, LANES), jnp.float32
    )

    @pl.when(me == 0)
    def _():
        field_ref[mine, 0:RIM] = jnp.zeros((RIM,) + field_ref.shape[2:], jnp.float32)

    @pl.when(me == slabs - 1)
    def _():
        field_ref[mine, RIM + rows :] = jnp.zeros((RIM,) + field_ref.shape[2:], jnp.float32)

    for copy in fetched[6:8]:
        copy.wait()
    square = variables * variables

    def select(pair, carry):
        for x0 in range(0, rows, 8):
            chosen = [jac_ref[k, pair, x0 : x0 + 8, :].astype(jnp.float32) for k in range(7)]
            codes = [codes_ref[k, x0 : x0 + 8, :] for k in range(7)]
            for code in range(9):
                value = jnp.zeros((8, LANES), jnp.float32)
                for k in range(7):
                    value = jnp.where(codes[k] == code, chosen[k], value)
                blocks[code * square + pair, x0 : x0 + 8, :] = value
        return carry

    lax.fori_loop(0, square, select, 0)

    total = square_row
    for k in range(slabs):
        if k > 0:
            copies[k - 1].wait_recv()
            total = total + recv_buf[k, data + 2 : data + 3]
        head, tail = split_2(recv_buf[k, 0:data])
        arrived[0:data, k * LANES : (k + 1) * LANES] = head
        arrived[data:, k * LANES : (k + 1) * LANES] = tail
        labels[0:1, k * LANES : (k + 1) * LANES] = recv_buf[k, data : data + 1].astype(jnp.int32)

    squares[0] = jnp.broadcast_to(total, (8, LANES))
    sq_copy = pltpu.make_async_remote_copy(
        src_ref=squares.at[0],
        dst_ref=squares.at[1],
        send_sem=sq_send,
        recv_sem=sq_recv,
        device_id={"cross": other},
        device_id_type=MESH,
    )
    sq_copy.start()

    cell_id = lax.broadcasted_iota(jnp.int32, (2 * LANES, slabs * LANES), 0)
    pairs = rows // 2

    def deposit(i, carry):
        pair = lax.rem(i + pairs - 3, pairs)
        hit = (labels[0:1, :] == cell_id + pair * (2 * LANES)).astype(jnp.float32)
        got = lax.dot_general(
            arrived[...], hit.astype(jnp.bfloat16), NT, preferred_element_type=jnp.float32
        )
        got = got[0:data] + got[data:]
        field_ref[mine, RIM + 2 * pair, 0:data, :] = got[:, 0:LANES]
        field_ref[mine, RIM + 2 * pair + 1, 0:data, :] = got[:, LANES:]
        return carry

    up = pltpu.make_async_remote_copy(
        src_ref=field_ref.at[mine, pl.ds(rows, RIM)],
        dst_ref=field_ref.at[mine, pl.ds(0, RIM)],
        send_sem=edge_send.at[0],
        recv_sem=edge_recv.at[0],
        device_id={"slab": lax.rem(me + 1, slabs)},
        device_id_type=MESH,
    )
    down = pltpu.make_async_remote_copy(
        src_ref=field_ref.at[mine, pl.ds(RIM, RIM)],
        dst_ref=field_ref.at[mine, pl.ds(RIM + rows, RIM)],
        send_sem=edge_send.at[1],
        recv_sem=edge_recv.at[1],
        device_id={"slab": lax.rem(me + slabs - 1, slabs)},
        device_id_type=MESH,
    )

    def across(n, start, size):
        return pltpu.make_async_remote_copy(
            src_ref=field_ref.at[mine, pl.ds(start, size)],
            dst_ref=field_ref.at[mine, pl.ds(start, size)],
            send_sem=pair_send.at[n],
            recv_sem=pair_recv.at[n],
            device_id={"cross": other},
            device_id_type=MESH,
        )

    middle = across(0, RIM, rows)
    low_rim = across(1, 0, RIM)
    high_rim = across(2, RIM + rows, RIM)

    lax.fori_loop(0, 3, deposit, 0)

    @pl.when(me < slabs - 1)
    def _():
        up.start()

    lax.fori_loop(3, 6, deposit, 0)

    @pl.when(me > 0)
    def _():
        down.start()

    lax.fori_loop(6, pairs, deposit, 0)
    middle.start()

    @pl.when(me > 0)
    def _():
        up.wait_recv()

    low_rim.start()

    @pl.when(me < slabs - 1)
    def _():
        down.wait_recv()

    high_rim.start()

    sq_copy.wait()
    whole = squares[0, 0:1] + squares[1, 0:1]
    lane = lax.broadcasted_iota(jnp.int32, (modes_dim, LANES), 1)
    mode = lax.broadcasted_iota(jnp.int32, (modes_dim, LANES), 0)
    per_mode = jnp.sum(
        jnp.where((lax.rem(lane, modes_dim) == mode) & (lane < data), whole, 0.0),
        axis=1,
        keepdims=True,
    )
    inverse = 1.0 / jnp.sqrt(per_mode / node_total + 1e-06)
    scale_ref[...] = jnp.broadcast_to(inverse, scale_ref.shape)

    middle.wait()
    low_rim.wait()
    high_rim.wait()

    planes = rows + 2 * RIM
    lane = lax.broadcasted_iota(jnp.int32, (modes_dim, LANES), 1)
    first, last = lane == 0, lane == LANES - 1

    def sweep(source, result, edge):
        def plane(x, carry):
            at = x - RIM + me * rows
            inside = ((at >= 0) & (at < slabs * rows)).astype(jnp.float32)
            for comp in range(comps):
                part = pl.ds(comp * modes_dim, modes_dim)
                left, right = source[0, x, part, :], source[1, x, part, :]
                left_up, right_up = pltpu.roll(left, 1, 1), pltpu.roll(right, 1, 1)
                left_down = pltpu.roll(left, LANES - 1, 1)
                right_down = pltpu.roll(right, LANES - 1, 1)
                near_left = jnp.where(first, 0.0, left_up) + jnp.where(last, right_down, left_down)
                near_right = jnp.where(first, left_up, right_up) + jnp.where(last, 0.0, right_down)
                for tile, near in ((0, near_left), (1, near_right)):
                    near = near + source[tile, x - 1, part, :] + source[tile, x + 1, part, :]
                    result[tile, x, part, :] = (
                        field_ref[tile, x, part, :] + SPREAD * near
                    ) * inside
            return carry

        lax.fori_loop(edge, planes - edge, plane, 0, unroll=2)

    sweep(field_ref, ping, 1)
    sweep(ping, pong, 2)
    sweep(pong, ping, 3)
    sweep(ping, pong, 4)

    here = (mine == 0).astype(jnp.float32)
    there = 1.0 - here

    def lift(x, carry):
        for b in range(variables):
            own = jnp.zeros((modes_dim, LANES), jnp.float32)
            far = jnp.zeros((modes_dim, LANES), jnp.float32)
            for comp in range(comps):
                part = pl.ds(comp * modes_dim, modes_dim)
                row = pl.ds(data + comp * variables + b, 1)
                own = own + field_ref[mine, x + RIM - 1, row, :] * pong[mine, x + RIM - 1, part, :]
                far = (
                    far + field_ref[other, x + RIM - 1, row, :] * pong[other, x + RIM - 1, part, :]
                )
            state[1, x, b] = own
            state[0, x, b] = jnp.where(first, pltpu.roll(far, 1, 1) * there, pltpu.roll(own, 1, 1))
            state[2, x, b] = jnp.where(
                last, pltpu.roll(far, LANES - 1, 1) * here, pltpu.roll(own, LANES - 1, 1)
            )
        return carry

    lax.fori_loop(0, rows + 2, lift, 0, unroll=2)

    stride = variables * rows

    def project(x, total):
        for b in range(variables):
            total = total + jnp.dot(
                pending[:, b * LANES : (b + 1) * LANES],
                pod_ref[b, x],
                preferred_element_type=jnp.float32,
            )
        return total

    def apply(x, total):
        total = project(jnp.maximum(x - 1, 0), total)
        sums = [jnp.zeros((modes_dim, LANES), jnp.float32) for _ in range(variables)]
        for code in range(9):
            for a in range(variables):
                value = state[code % 3, x + code // 3, a]
                for b in range(variables):
                    gain = blocks[code * square + b * variables + a, pl.ds(x, 1), :]
                    sums[b] = sums[b] + gain * value
        for b in range(variables):
            result = sums[b] * scale_ref[...]
            induced_ref[pl.ds(b * rows + x, modes_dim, stride=stride), :] = result
            high, low = split_2(result)
            pending[0:modes_dim, b * LANES : (b + 1) * LANES] = high
            pending[modes_dim:, b * LANES : (b + 1) * LANES] = low
        return total

    fetched[8].wait()
    pending[...] = jnp.zeros(pending.shape, jnp.bfloat16)
    total = lax.fori_loop(
        0, rows, apply, jnp.zeros((2 * modes_dim, reduced_ref.shape[1]), jnp.float32)
    )
    total = project(rows - 1, total)
    result = total[0:modes_dim] + total[modes_dim:]
    share = modes_dim // count
    for n in range(count):
        part_ref[n] = result[n * share : (n + 1) * share]
    written = pltpu.make_async_copy(induced_ref, induced_hbm, out_sem)
    written.start()
    parts = []
    for k in range(1, count):
        at, device = peer(k)
        copy = pltpu.make_async_remote_copy(
            src_ref=part_ref.at[at],
            dst_ref=got.at[k],
            send_sem=part_send.at[k],
            recv_sem=part_recv.at[k],
            device_id=device,
            device_id_type=MESH,
        )
        copy.start()
        parts.append(copy)
    total = part_ref[rank_here]
    for k in range(1, count):
        parts[k - 1].wait_recv()
        total = total + got[k]
    mine_sum[...] = total
    sum_ref[rank_here] = total
    backs = []
    for k in range(1, count):
        _, device = peer(k)
        copy = pltpu.make_async_remote_copy(
            src_ref=mine_sum,
            dst_ref=sum_ref.at[rank_here],
            send_sem=back_send.at[k],
            recv_sem=back_recv.at[k],
            device_id=device,
            device_id_type=MESH,
        )
        copy.start()
        backs.append(copy)
    for copy in parts:
        copy.wait_send()
    for copy in backs:
        copy.wait()
    for n in range(count):
        reduced_ref[n * share : (n + 1) * share, :] = sum_ref[n]
    for copy in copies:
        copy.wait_send()

    @pl.when(me < slabs - 1)
    def _():
        up.wait_send()

    @pl.when(me > 0)
    def _():
        down.wait_send()
    written.wait()


VMEM = pl.BlockSpec(memory_space=pltpu.VMEM)

ANY = pl.BlockSpec(memory_space=pl.ANY)


def fast_body(
    mode_shapes,
    stencil,
    stencil_weight,
    owner_slab,
    target_cell,
    neighbour_codes,
    jacobian,
    lift_matrix,
    pod_basis,
):
    slabs = lax.axis_size("slab")
    crosses = lax.axis_size("cross")
    modes_dim, comps, nodes = mode_shapes.shape
    surf = owner_slab.shape[0]
    rows, cols = neighbour_codes.shape[1:]
    variables = lift_matrix.shape[0]
    pod = pod_basis.shape[-1]
    data = modes_dim * comps
    planes = rows + 2 * RIM
    count = slabs * crosses
    share = modes_dim // count
    dma = pltpu.SemaphoreType.DMA
    operands = (
        mode_shapes.transpose(1, 0, 2).reshape(data, nodes),
        stencil,
        stencil_weight,
        owner_slab.reshape(1, surf),
        target_cell.reshape(1, surf),
        lift_matrix,
        neighbour_codes,
        jacobian.reshape(jacobian.shape[0], variables * variables, rows, cols),
        pod_basis,
    )
    sweep_shape = pltpu.VMEM((crosses, planes, data, cols), jnp.float32)
    induced, reduced = pl.pallas_call(
        functools.partial(
            whole_kernel,
            slabs,
            rows,
            modes_dim,
            comps,
            variables,
            float(comps * nodes * count),
        ),
        out_shape=(
            jax.ShapeDtypeStruct((modes_dim * variables * rows, cols), jnp.float32),
            jax.ShapeDtypeStruct((modes_dim, pod), jnp.float32),
        ),
        in_specs=[ANY] * len(operands),
        out_specs=(ANY, VMEM),
        scratch_shapes=[pltpu.VMEM(x.shape, x.dtype) for x in operands[1:]]
        + [
            pltpu.VMEM((LANES, nodes), jnp.float32),
            pltpu.VMEM((crosses, planes, data + 16, cols), jnp.float32),
            pltpu.VMEM((modes_dim, LANES), jnp.float32),
            pltpu.VMEM((slabs, data + 8, LANES), jnp.float32),
            pltpu.VMEM((slabs, data + 8, LANES), jnp.float32),
            pltpu.VMEM((2 * data, slabs * LANES), jnp.bfloat16),
            pltpu.VMEM((8, slabs * LANES), jnp.int32),
            pltpu.VMEM((2, 8, LANES), jnp.float32),
            sweep_shape,
            sweep_shape,
            pltpu.VMEM((3, rows + 2, variables, modes_dim, cols), jnp.float32),
            pltpu.VMEM((9 * variables * variables, rows, cols), jnp.float32),
            pltpu.VMEM((2 * modes_dim, variables * cols), jnp.bfloat16),
            pltpu.VMEM((modes_dim * variables * rows, cols), jnp.float32),
            pltpu.VMEM((count, share, pod), jnp.float32),
            pltpu.VMEM((count, share, pod), jnp.float32),
            pltpu.VMEM((share, pod), jnp.float32),
            pltpu.VMEM((count, share, pod), jnp.float32),
            dma((len(operands),)),
            dma,
            dma((slabs,)),
            dma((slabs,)),
            dma((2,)),
            dma((2,)),
            dma((3,)),
            dma((3,)),
            dma,
            dma,
            dma((count,)),
            dma((count,)),
            dma((count,)),
            dma((count,)),
        ],
        compiler_params=pltpu.CompilerParams(
            collective_id=0, has_side_effects=True, vmem_limit_bytes=56 * 1024 * 1024
        ),
    )(*operands)
    return induced.reshape(modes_dim, variables, rows, cols), reduced


def padded_2(block, sides, width):
    for axis, dim in sides:
        count = lax.axis_size(axis)
        forward = [(i, i + 1) for i in range(count - 1)]
        backward = [(target, source) for source, target in forward]
        low = lax.ppermute(
            lax.slice_in_dim(block, block.shape[dim] - width, None, axis=dim), axis, forward
        )
        high = lax.ppermute(lax.slice_in_dim(block, 0, width, axis=dim), axis, backward)
        block = jnp.concatenate([low, block, high], axis=dim)
    return block


def lift_state(lift_gain, field_now):
    accumulated = 0.0
    for component in range(lift_gain.shape[1]):
        accumulated = accumulated + lift_gain[:, component] * jnp.expand_dims(
            field_now[..., component, :, :], -3
        )
    return accumulated


def offset_blocks(codes, jacobian):
    zero_block = jnp.zeros((), jnp.bfloat16)
    stacked = []
    for offset_code in range(9):
        chosen = jnp.where((codes == offset_code)[:, None, None], jacobian, zero_block)
        stacked.append(jnp.sum(chosen, axis=0, dtype=jnp.float32))
    return jnp.stack(stacked)


def apply_blocks(blocks, padded, cell_rows, cell_cols):
    accumulated = 0.0
    for offset_code in range(9):
        start_x = offset_code // 3
        start_y = offset_code % 3
        shifted = padded[..., start_x : start_x + cell_rows, start_y : start_y + cell_cols]
        for component in range(blocks.shape[2]):
            accumulated = accumulated + blocks[offset_code, :, component] * jnp.expand_dims(
                shifted[..., component, :, :], -3
            )
    return accumulated


def body(
    mode_shapes,
    stencil,
    stencil_weight,
    owner_slab,
    target_cell,
    neighbour_codes,
    jacobian,
    lift_matrix,
    pod_basis,
):
    slab_count = lax.axis_size("slab")
    cross_count = lax.axis_size("cross")
    mode_count, space_dims, nodes_dev = mode_shapes.shape
    surf_dev = owner_slab.shape[0]
    capacity = 2 * surf_dev // slab_count
    cell_rows = neighbour_codes.shape[1]
    cell_cols = neighbour_codes.shape[2]
    total_nodes = nodes_dev * slab_count * cross_count
    squares = jnp.sum(mode_shapes * mode_shapes, axis=(1, 2))
    scale_rms = jnp.sqrt(lax.psum(squares, ("slab", "cross")) / (space_dims * total_nodes) + 1e-06)
    shapes_used = mode_shapes / scale_rms[:, None, None]
    picked = shapes_used[:, :, stencil]
    surface = jnp.sum(stencil_weight[None, None] * picked, axis=2)
    dest_slab = owner_slab[:, 0]
    onehot = (dest_slab[:, None] == jnp.arange(slab_count, dtype=jnp.int32)[None, :]).astype(
        jnp.int32
    )
    slot_rank = jnp.sum((jnp.cumsum(onehot, axis=0) - 1) * onehot, axis=1)
    position = dest_slab * capacity + slot_rank
    payload = jnp.zeros((mode_count * space_dims, slab_count * capacity), jnp.float32)
    payload = payload.at[:, position].set(surface.reshape(mode_count * space_dims, surf_dev))
    labels = jnp.zeros((1, slab_count * capacity), jnp.int32).at[0, position].set(target_cell)
    arrived, arrived_cells = (
        lax.all_to_all(payload, "slab", split_axis=1, concat_axis=1, tiled=True),
        lax.all_to_all(labels, "slab", split_axis=1, concat_axis=1, tiled=True),
    )
    deposit = jnp.zeros((mode_count * space_dims, cell_rows * cell_cols), jnp.float32)
    deposit = (
        deposit.at[:, arrived_cells[0]]
        .add(arrived)
        .reshape(mode_count, space_dims, cell_rows, cell_cols)
    )
    rim_width = SWEEPS + 1
    source_padded = padded_2(deposit, (("slab", 2), ("cross", 3)), rim_width)
    grid_x = (
        lax.axis_index("slab") * cell_rows
        - rim_width
        + jnp.arange(cell_rows + 2 * rim_width, dtype=jnp.int32)
    )
    grid_y = (
        lax.axis_index("cross") * cell_cols
        - rim_width
        + jnp.arange(cell_cols + 2 * rim_width, dtype=jnp.int32)
    )
    inside_x = (grid_x >= 0) & (grid_x < cell_rows * slab_count)
    inside_y = (grid_y >= 0) & (grid_y < cell_cols * cross_count)
    inside_mask = (inside_x[:, None] & inside_y[None, :]).astype(jnp.float32)
    field_now = source_padded
    for sweep_index in range(SWEEPS):
        edge_start = sweep_index + 1
        upper_x = cell_rows + 2 * rim_width - edge_start
        upper_y = cell_cols + 2 * rim_width - edge_start
        neighbours = (
            field_now[..., 2:, 1:-1]
            + field_now[..., :-2, 1:-1]
            + field_now[..., 1:-1, 2:]
            + field_now[..., 1:-1, :-2]
        )
        field_now = (
            source_padded[..., edge_start:upper_x, edge_start:upper_y] + SPREAD * neighbours
        ) * inside_mask[edge_start:upper_x, edge_start:upper_y]
    lift_padded = padded_2(lift_matrix, (("slab", 2), ("cross", 3)), 1)
    state_padded = lift_state(lift_padded.astype(jnp.float32), field_now)
    blocks = offset_blocks(neighbour_codes, jacobian)
    induced = apply_blocks(blocks, state_padded, cell_rows, cell_cols)
    partial_value = jnp.dot(
        induced.reshape(mode_count, -1),
        pod_basis.reshape(-1, pod_basis.shape[-1]),
        precision=lax.Precision.HIGHEST,
        preferred_element_type=jnp.float32,
    )
    reduced = lax.psum(partial_value, ("slab", "cross"))
    return (induced, reduced)


def solution(mesh):
    in_specs = (
        P(None, None, ("slab", "cross")),
        P(None, ("slab", "cross")),
        P(None, ("slab", "cross")),
        P(("slab", "cross"), None),
        P(("slab", "cross")),
        P(None, "slab", "cross"),
        P("groups", None, None, "slab", "cross"),
        P("groups", None, "slab", "cross"),
        P("groups", "slab", "cross", None),
    )
    out_specs = (P("groups", None, "slab", "cross"), P("groups", None))
    slabs, crosses = mesh.shape["slab"], mesh.shape["cross"]
    chosen = fast_body if crosses == 2 and slabs == 8 else body
    return jax.shard_map(chosen, mesh=mesh, in_specs=in_specs, out_specs=out_specs, check_vma=False)
```

```python
import functools

import jax
import jax.numpy as jnp
from jax import lax
from jax.experimental import pallas as pl
from jax.experimental.pallas import tpu as pltpu
from jax.sharding import PartitionSpec as P

SWEEPS = 4


SPREAD = 0.24

RIM = SWEEPS + 1

LANES = 128

MESH = pl.DeviceIdType.MESH

NT = (((1,), (1,)), ((), ()))


def split_2(value):
    high = value.astype(jnp.bfloat16)
    low = (value - high.astype(jnp.float32)).astype(jnp.bfloat16)
    return high, low


def whole_kernel(
    slabs,
    rows,
    modes_dim,
    comps,
    variables,
    node_total,
    shapes_hbm,
    stencil_hbm,
    weight_hbm,
    owner_hbm,
    target_hbm,
    lift_hbm,
    codes_hbm,
    jac_hbm,
    pod_hbm,
    induced_ref,
    reduced_ref,
    stencil_ref,
    weight_ref,
    owner_ref,
    target_ref,
    lift_ref,
    codes_ref,
    jac_ref,
    pod_ref,
    modes_ref,
    field_ref,
    scale_ref,
    send_buf,
    recv_buf,
    arrived,
    labels,
    squares,
    field_1,
    field_2,
    field_3,
    field_4,
    state,
    blocks,
    pending,
    part_ref,
    pair_part,
    chip_sum,
    got,
    sum_ref,
    fetch_sem,
    send_sem,
    recv_sem,
    edge_send,
    edge_recv,
    pair_send,
    pair_recv,
    sq_send,
    sq_recv,
    part_send,
    part_recv,
    back_send,
    back_recv,
):
    me = lax.axis_index("slab")
    mine = lax.axis_index("cross")
    other = 1 - mine
    nodes = modes_ref.shape[1]
    data = modes_dim * comps
    surf = stencil_ref.shape[1]

    fetched = [
        pltpu.make_async_copy(source, held, fetch_sem.at[n])
        for n, (source, held) in enumerate(
            (
                (shapes_hbm, modes_ref.at[pl.ds(0, data)]),
                (stencil_hbm, stencil_ref),
                (weight_hbm, weight_ref),
                (owner_hbm, owner_ref),
                (target_hbm, target_ref),
                (lift_hbm, lift_ref),
                (codes_hbm, codes_ref),
                (jac_hbm, jac_ref),
                (pod_hbm, pod_ref),
            )
        )
    ]
    for copy in fetched:
        copy.start()

    barrier = pltpu.get_barrier_semaphore()
    for k in range(1, slabs):
        pl.semaphore_signal(
            barrier, inc=1, device_id={"slab": lax.rem(me + k, slabs)}, device_id_type=MESH
        )
    pl.semaphore_signal(barrier, inc=1, device_id={"cross": other}, device_id_type=MESH)

    for copy in fetched[0:6]:
        copy.wait()
    modes_ref[data:, :] = jnp.zeros((LANES - data, nodes), jnp.float32)

    node_id = lax.broadcasted_iota(jnp.int32, (nodes, surf), 0)
    mix = jnp.zeros((nodes, surf), jnp.float32)
    for j in range(stencil_ref.shape[0]):
        mix = mix + jnp.where(stencil_ref[j : j + 1, :] == node_id, weight_ref[j : j + 1, :], 0.0)
    surface = jnp.dot(
        modes_ref[...], mix, precision=lax.Precision.HIGHEST, preferred_element_type=jnp.float32
    )
    owner = owner_ref[...]
    slab_id = lax.broadcasted_iota(jnp.int32, (slabs, surf), 0)
    named = (owner == slab_id).astype(jnp.float32)
    before = (
        lax.broadcasted_iota(jnp.int32, (surf, surf), 0)
        < lax.broadcasted_iota(jnp.int32, (surf, surf), 1)
    ).astype(jnp.bfloat16)
    ahead = jnp.dot(named.astype(jnp.bfloat16), before, preferred_element_type=jnp.float32)
    rank = jnp.sum(ahead * named, axis=0, keepdims=True).astype(jnp.int32)
    position = owner * LANES + rank
    target = target_ref[...]
    target_low = lax.rem(target, 64)
    row_id = lax.broadcasted_iota(jnp.int32, surface.shape, 0)
    high = surface.astype(jnp.bfloat16).astype(jnp.float32)
    low = surface - high
    high = jnp.where(row_id == data, (target - target_low).astype(jnp.float32), high)
    high = jnp.where(row_id == data + 1, 1.0, high)
    low = jnp.where(row_id == data, target_low.astype(jnp.float32), low)
    both = jnp.concatenate([high, low], axis=0).astype(jnp.bfloat16)
    modes = modes_ref[...]
    square_row = lax.dot_general(
        jnp.ones((8, nodes), jnp.float32),
        modes * modes,
        NT,
        precision=lax.Precision.HIGHEST,
        preferred_element_type=jnp.float32,
    )[0:1]
    slot_id = lax.broadcasted_iota(jnp.int32, (LANES, surf), 0)
    out_rows = send_buf.shape[1]
    out_id = lax.broadcasted_iota(jnp.int32, (out_rows, LANES), 0)

    pl.semaphore_wait(barrier, slabs)
    copies = []
    for step in range(slabs):
        k = (step + 1) % slabs
        dest = lax.rem(me + k, slabs)
        onehot = (position == slot_id + dest * LANES).astype(jnp.float32).astype(jnp.bfloat16)
        packed = lax.dot_general(both, onehot, NT, preferred_element_type=jnp.float32)
        block = packed[0:out_rows] + packed[LANES : LANES + out_rows]
        empty = 1.0 - block[data + 1 : data + 2]
        block = jnp.where(out_id == data, block - 65536.0 * empty, block)
        block = jnp.where(out_id == data + 2, square_row, block)
        if k == 0:
            recv_buf[0] = block
        else:
            send_buf[k] = block
            copy = pltpu.make_async_remote_copy(
                src_ref=send_buf.at[k],
                dst_ref=recv_buf.at[k],
                send_sem=send_sem.at[k],
                recv_sem=recv_sem.at[k],
                device_id={"slab": dest},
                device_id_type=MESH,
            )
            copy.start()
            copies.append(copy)

    for comp in range(comps):
        for b in range(variables):
            field_ref[mine, RIM : RIM + rows, data + comp * variables + b, :] = lift_ref[
                b, comp
            ].astype(jnp.float32)
    field_ref[mine, RIM : RIM + rows, data + comps * variables, :] = jnp.zeros(
        (rows, LANES), jnp.float32
    )

    @pl.when(me == 0)
    def _():
        field_ref[mine, 0:RIM] = jnp.zeros((RIM,) + field_ref.shape[2:], jnp.float32)

    @pl.when(me == slabs - 1)
    def _():
        field_ref[mine, RIM + rows :] = jnp.zeros((RIM,) + field_ref.shape[2:], jnp.float32)

    for copy in fetched[6:8]:
        copy.wait()
    square = variables * variables

    def select(pair, carry):
        for x0 in range(0, rows, 8):
            chosen = [jac_ref[k, pair, x0 : x0 + 8, :].astype(jnp.float32) for k in range(7)]
            codes = [codes_ref[k, x0 : x0 + 8, :] for k in range(7)]
            for code in range(9):
                value = jnp.zeros((8, LANES), jnp.float32)
                for k in range(7):
                    value = jnp.where(codes[k] == code, chosen[k], value)
                blocks[code * square + pair, x0 : x0 + 8, :] = value
        return carry

    lax.fori_loop(0, square, select, 0)

    total = square_row
    for k in range(slabs):
        if k > 0:
            copies[k - 1].wait_recv()
            total = total + recv_buf[k, data + 2 : data + 3]
        head, tail = split_2(recv_buf[k, 0:data])
        arrived[0:data, k * LANES : (k + 1) * LANES] = head
        arrived[data:, k * LANES : (k + 1) * LANES] = tail
        labels[0:1, k * LANES : (k + 1) * LANES] = recv_buf[k, data : data + 1].astype(jnp.int32)

    squares[0] = jnp.broadcast_to(total, (8, LANES))
    sq_copy = pltpu.make_async_remote_copy(
        src_ref=squares.at[0],
        dst_ref=squares.at[1],
        send_sem=sq_send,
        recv_sem=sq_recv,
        device_id={"cross": other},
        device_id_type=MESH,
    )
    sq_copy.start()

    cell_id = lax.broadcasted_iota(jnp.int32, (2 * LANES, slabs * LANES), 0)
    pairs = rows // 2

    def deposit(i, carry):
        pair = lax.rem(i + pairs - 3, pairs)
        hit = (labels[0:1, :] == cell_id + pair * (2 * LANES)).astype(jnp.float32)
        got = lax.dot_general(
            arrived[...], hit.astype(jnp.bfloat16), NT, preferred_element_type=jnp.float32
        )
        got = got[0:data] + got[data:]
        field_ref[mine, RIM + 2 * pair, 0:data, :] = got[:, 0:LANES]
        field_ref[mine, RIM + 2 * pair + 1, 0:data, :] = got[:, LANES:]
        return carry

    up = pltpu.make_async_remote_copy(
        src_ref=field_ref.at[mine, pl.ds(rows, RIM)],
        dst_ref=field_ref.at[mine, pl.ds(0, RIM)],
        send_sem=edge_send.at[0],
        recv_sem=edge_recv.at[0],
        device_id={"slab": lax.rem(me + 1, slabs)},
        device_id_type=MESH,
    )
    down = pltpu.make_async_remote_copy(
        src_ref=field_ref.at[mine, pl.ds(RIM, RIM)],
        dst_ref=field_ref.at[mine, pl.ds(RIM + rows, RIM)],
        send_sem=edge_send.at[1],
        recv_sem=edge_recv.at[1],
        device_id={"slab": lax.rem(me + slabs - 1, slabs)},
        device_id_type=MESH,
    )

    def across(n, start, size):
        return pltpu.make_async_remote_copy(
            src_ref=field_ref.at[mine, pl.ds(start, size)],
            dst_ref=field_ref.at[mine, pl.ds(start, size)],
            send_sem=pair_send.at[n],
            recv_sem=pair_recv.at[n],
            device_id={"cross": other},
            device_id_type=MESH,
        )

    third = (pairs - 6) // 2
    middle = [
        across(0, RIM + rows - 6, 6),
        across(1, RIM, 6),
        across(2, RIM + 6, 2 * third),
        across(3, RIM + 6 + 2 * third, rows - 12 - 2 * third),
    ]
    low_rim = across(4, 0, RIM)
    high_rim = across(5, RIM + rows, RIM)

    lax.fori_loop(0, 3, deposit, 0)

    @pl.when(me < slabs - 1)
    def _():
        up.start()

    middle[0].start()
    lax.fori_loop(3, 6, deposit, 0)

    @pl.when(me > 0)
    def _():
        down.start()

    middle[1].start()
    lax.fori_loop(6, 6 + third, deposit, 0)
    middle[2].start()
    lax.fori_loop(6 + third, pairs, deposit, 0)
    middle[3].start()

    sq_copy.wait()
    whole = squares[0, 0:1] + squares[1, 0:1]
    lane = lax.broadcasted_iota(jnp.int32, (modes_dim, LANES), 1)
    mode = lax.broadcasted_iota(jnp.int32, (modes_dim, LANES), 0)
    per_mode = jnp.sum(
        jnp.where((lax.rem(lane, modes_dim) == mode) & (lane < data), whole, 0.0),
        axis=1,
        keepdims=True,
    )
    inverse = 1.0 / jnp.sqrt(per_mode / node_total + 1e-06)
    scale_ref[...] = jnp.broadcast_to(inverse, scale_ref.shape)

    planes = rows + 2 * RIM
    lane = lax.broadcasted_iota(jnp.int32, (modes_dim, LANES), 1)
    first, last = lane == 0, lane == LANES - 1

    def sweep(source, result, x, inside):
        for comp in range(comps):
            part = pl.ds(comp * modes_dim, modes_dim)
            left, right = source[0, x, part, :], source[1, x, part, :]
            near_left = pltpu.roll(jnp.where(last, 0.0, left), 1, 1) + pltpu.roll(
                jnp.where(first, right, left), LANES - 1, 1
            )
            near_right = pltpu.roll(jnp.where(last, left, right), 1, 1) + pltpu.roll(
                jnp.where(first, 0.0, right), LANES - 1, 1
            )
            for tile, near in ((0, near_left), (1, near_right)):
                near = near + source[tile, x - 1, part, :] + source[tile, x + 1, part, :]
                value = field_ref[tile, x, part, :] + SPREAD * near
                result[tile, x, part, :] = value if inside is None else value * inside

    fields = [field_1, field_2, field_3, field_4]
    stages = [field_ref, *fields]

    def inner(step):
        def plane(x, carry):
            sweep(stages[step - 1], stages[step], x, None)
            return carry

        lax.fori_loop(RIM + step, RIM + rows - step, plane, 0, unroll=2)

    def outer(step):
        def plane(i, carry):
            for x in (step + i, planes - RIM - step + i):
                at = x - RIM + me * rows
                inside = ((at >= 0) & (at < slabs * rows)).astype(jnp.float32)
                sweep(stages[step - 1], stages[step], x, inside)
            return carry

        lax.fori_loop(0, RIM, plane, 0)

    for copy in middle:
        copy.wait_recv()
    for step in range(1, SWEEPS):
        inner(step)

    @pl.when(me > 0)
    def _():
        up.wait_recv()

    low_rim.start()

    @pl.when(me < slabs - 1)
    def _():
        down.wait_recv()

    high_rim.start()
    inner(SWEEPS)
    low_rim.wait_recv()
    high_rim.wait_recv()
    for step in range(1, SWEEPS + 1):
        outer(step)
    pong = fields[SWEEPS - 1]

    here = (mine == 0).astype(jnp.float32)
    there = 1.0 - here

    def lift(x, carry):
        for b in range(variables):
            own = jnp.zeros((modes_dim, LANES), jnp.float32)
            far = jnp.zeros((modes_dim, LANES), jnp.float32)
            for comp in range(comps):
                part = pl.ds(comp * modes_dim, modes_dim)
                row = pl.ds(data + comp * variables + b, 1)
                own = own + field_ref[mine, x + RIM - 1, row, :] * pong[mine, x + RIM - 1, part, :]
                far = (
                    far + field_ref[other, x + RIM - 1, row, :] * pong[other, x + RIM - 1, part, :]
                )
            state[1, x, b] = own
            state[0, x, b] = pltpu.roll(jnp.where(last, far * there, own), 1, 1)
            state[2, x, b] = pltpu.roll(jnp.where(first, far * here, own), LANES - 1, 1)
        return carry

    lax.fori_loop(0, rows + 2, lift, 0, unroll=2)

    stride = variables * rows

    def project(x, total):
        for b in range(variables):
            total = total + jnp.dot(
                pending[:, b * LANES : (b + 1) * LANES],
                pod_ref[b, x],
                preferred_element_type=jnp.float32,
            )
        return total

    def apply(x, total):
        total = project(jnp.maximum(x - 1, 0), total)
        sums = [jnp.zeros((modes_dim, LANES), jnp.float32) for _ in range(variables)]
        for code in range(9):
            for a in range(variables):
                value = state[code % 3, x + code // 3, a]
                for b in range(variables):
                    gain = blocks[code * square + b * variables + a, pl.ds(x, 1), :]
                    sums[b] = sums[b] + gain * value
        for b in range(variables):
            result = sums[b] * scale_ref[...]
            induced_ref[pl.ds(b * rows + x, modes_dim, stride=stride), :] = result
            high, low = split_2(result)
            pending[0:modes_dim, b * LANES : (b + 1) * LANES] = high
            pending[modes_dim:, b * LANES : (b + 1) * LANES] = low
        return total

    fetched[8].wait()
    pending[...] = jnp.zeros(pending.shape, jnp.bfloat16)
    total = lax.fori_loop(
        0, rows, apply, jnp.zeros((2 * modes_dim, reduced_ref.shape[1]), jnp.float32), unroll=2
    )
    total = project(rows - 1, total)
    result = total[0:modes_dim] + total[modes_dim:]
    half = modes_dim // 2
    part_ref[0] = result[0:half]
    part_ref[1] = result[half:]
    to_pair = pltpu.make_async_remote_copy(
        src_ref=part_ref.at[other],
        dst_ref=pair_part,
        send_sem=back_send.at[0],
        recv_sem=back_recv.at[0],
        device_id={"cross": other},
        device_id_type=MESH,
    )
    to_pair.start()
    to_pair.wait()
    chip_sum[...] = part_ref[mine] + pair_part[...]
    parts = []
    for k in range(1, slabs):
        copy = pltpu.make_async_remote_copy(
            src_ref=chip_sum,
            dst_ref=got.at[me],
            send_sem=part_send.at[k],
            recv_sem=part_recv.at[k],
            device_id={"slab": lax.rem(me + k, slabs)},
            device_id_type=MESH,
        )
        copy.start()
        parts.append(copy)
    got[me] = chip_sum[...]
    for copy in parts:
        copy.wait()
    whole_sum = got[0]
    for n in range(1, slabs):
        whole_sum = whole_sum + got[n]
    sum_ref[mine] = whole_sum
    back = pltpu.make_async_remote_copy(
        src_ref=sum_ref.at[mine],
        dst_ref=sum_ref.at[mine],
        send_sem=back_send.at[1],
        recv_sem=back_recv.at[1],
        device_id={"cross": other},
        device_id_type=MESH,
    )
    back.start()
    back.wait()
    reduced_ref[0:half, :] = sum_ref[0]
    reduced_ref[half:, :] = sum_ref[1]
    for copy in middle:
        copy.wait_send()
    low_rim.wait_send()
    high_rim.wait_send()
    for copy in copies:
        copy.wait_send()

    @pl.when(me < slabs - 1)
    def _():
        up.wait_send()

    @pl.when(me > 0)
    def _():
        down.wait_send()


VMEM = pl.BlockSpec(memory_space=pltpu.VMEM)

ANY = pl.BlockSpec(memory_space=pl.ANY)


def fast_body(
    mode_shapes,
    stencil,
    stencil_weight,
    owner_slab,
    target_cell,
    neighbour_codes,
    jacobian,
    lift_matrix,
    pod_basis,
):
    slabs = lax.axis_size("slab")
    crosses = lax.axis_size("cross")
    modes_dim, comps, nodes = mode_shapes.shape
    surf = owner_slab.shape[0]
    rows, cols = neighbour_codes.shape[1:]
    variables = lift_matrix.shape[0]
    pod = pod_basis.shape[-1]
    data = modes_dim * comps
    planes = rows + 2 * RIM
    count = slabs * crosses
    half = modes_dim // 2
    dma = pltpu.SemaphoreType.DMA
    operands = (
        mode_shapes.transpose(1, 0, 2).reshape(data, nodes),
        stencil,
        stencil_weight,
        owner_slab.reshape(1, surf),
        target_cell.reshape(1, surf),
        lift_matrix,
        neighbour_codes,
        jacobian.reshape(jacobian.shape[0], variables * variables, rows, cols),
        pod_basis,
    )
    sweep_shape = pltpu.VMEM((crosses, planes, data, cols), jnp.float32)
    induced, reduced = pl.pallas_call(
        functools.partial(
            whole_kernel,
            slabs,
            rows,
            modes_dim,
            comps,
            variables,
            float(comps * nodes * count),
        ),
        out_shape=(
            jax.ShapeDtypeStruct((modes_dim * variables * rows, cols), jnp.float32),
            jax.ShapeDtypeStruct((modes_dim, pod), jnp.float32),
        ),
        in_specs=[ANY] * len(operands),
        out_specs=(VMEM, VMEM),
        scratch_shapes=[pltpu.VMEM(x.shape, x.dtype) for x in operands[1:]]
        + [
            pltpu.VMEM((LANES, nodes), jnp.float32),
            pltpu.VMEM((crosses, planes, data + 16, cols), jnp.float32),
            pltpu.VMEM((modes_dim, LANES), jnp.float32),
            pltpu.VMEM((slabs, data + 8, LANES), jnp.float32),
            pltpu.VMEM((slabs, data + 8, LANES), jnp.float32),
            pltpu.VMEM((2 * data, slabs * LANES), jnp.bfloat16),
            pltpu.VMEM((8, slabs * LANES), jnp.int32),
            pltpu.VMEM((2, 8, LANES), jnp.float32),
            sweep_shape,
            sweep_shape,
            sweep_shape,
            sweep_shape,
            pltpu.VMEM((3, rows + 2, variables, modes_dim, cols), jnp.float32),
            pltpu.VMEM((9 * variables * variables, rows, cols), jnp.float32),
            pltpu.VMEM((2 * modes_dim, variables * cols), jnp.bfloat16),
            pltpu.VMEM((2, half, pod), jnp.float32),
            pltpu.VMEM((half, pod), jnp.float32),
            pltpu.VMEM((half, pod), jnp.float32),
            pltpu.VMEM((slabs, half, pod), jnp.float32),
            pltpu.VMEM((2, half, pod), jnp.float32),
            dma((len(operands),)),
            dma((slabs,)),
            dma((slabs,)),
            dma((2,)),
            dma((2,)),
            dma((6,)),
            dma((6,)),
            dma,
            dma,
            dma((slabs,)),
            dma((slabs,)),
            dma((2,)),
            dma((2,)),
        ],
        compiler_params=pltpu.CompilerParams(
            collective_id=0, has_side_effects=True, vmem_limit_bytes=56 * 1024 * 1024
        ),
    )(*operands)
    return induced.reshape(modes_dim, variables, rows, cols), reduced


def padded_2(block, sides, width):
    for axis, dim in sides:
        count = lax.axis_size(axis)
        forward = [(i, i + 1) for i in range(count - 1)]
        backward = [(target, source) for source, target in forward]
        low = lax.ppermute(
            lax.slice_in_dim(block, block.shape[dim] - width, None, axis=dim), axis, forward
        )
        high = lax.ppermute(lax.slice_in_dim(block, 0, width, axis=dim), axis, backward)
        block = jnp.concatenate([low, block, high], axis=dim)
    return block


def lift_state(lift_gain, field_now):
    accumulated = 0.0
    for component in range(lift_gain.shape[1]):
        accumulated = accumulated + lift_gain[:, component] * jnp.expand_dims(
            field_now[..., component, :, :], -3
        )
    return accumulated


def offset_blocks(codes, jacobian):
    zero_block = jnp.zeros((), jnp.bfloat16)
    stacked = []
    for offset_code in range(9):
        chosen = jnp.where((codes == offset_code)[:, None, None], jacobian, zero_block)
        stacked.append(jnp.sum(chosen, axis=0, dtype=jnp.float32))
    return jnp.stack(stacked)


def apply_blocks(blocks, padded, cell_rows, cell_cols):
    accumulated = 0.0
    for offset_code in range(9):
        start_x = offset_code // 3
        start_y = offset_code % 3
        shifted = padded[..., start_x : start_x + cell_rows, start_y : start_y + cell_cols]
        for component in range(blocks.shape[2]):
            accumulated = accumulated + blocks[offset_code, :, component] * jnp.expand_dims(
                shifted[..., component, :, :], -3
            )
    return accumulated


def body(
    mode_shapes,
    stencil,
    stencil_weight,
    owner_slab,
    target_cell,
    neighbour_codes,
    jacobian,
    lift_matrix,
    pod_basis,
):
    slab_count = lax.axis_size("slab")
    cross_count = lax.axis_size("cross")
    mode_count, space_dims, nodes_dev = mode_shapes.shape
    surf_dev = owner_slab.shape[0]
    capacity = 2 * surf_dev // slab_count
    cell_rows = neighbour_codes.shape[1]
    cell_cols = neighbour_codes.shape[2]
    total_nodes = nodes_dev * slab_count * cross_count
    squares = jnp.sum(mode_shapes * mode_shapes, axis=(1, 2))
    scale_rms = jnp.sqrt(lax.psum(squares, ("slab", "cross")) / (space_dims * total_nodes) + 1e-06)
    shapes_used = mode_shapes / scale_rms[:, None, None]
    picked = shapes_used[:, :, stencil]
    surface = jnp.sum(stencil_weight[None, None] * picked, axis=2)
    dest_slab = owner_slab[:, 0]
    onehot = (dest_slab[:, None] == jnp.arange(slab_count, dtype=jnp.int32)[None, :]).astype(
        jnp.int32
    )
    slot_rank = jnp.sum((jnp.cumsum(onehot, axis=0) - 1) * onehot, axis=1)
    position = dest_slab * capacity + slot_rank
    payload = jnp.zeros((mode_count * space_dims, slab_count * capacity), jnp.float32)
    payload = payload.at[:, position].set(surface.reshape(mode_count * space_dims, surf_dev))
    labels = jnp.zeros((1, slab_count * capacity), jnp.int32).at[0, position].set(target_cell)
    arrived, arrived_cells = (
        lax.all_to_all(payload, "slab", split_axis=1, concat_axis=1, tiled=True),
        lax.all_to_all(labels, "slab", split_axis=1, concat_axis=1, tiled=True),
    )
    deposit = jnp.zeros((mode_count * space_dims, cell_rows * cell_cols), jnp.float32)
    deposit = (
        deposit.at[:, arrived_cells[0]]
        .add(arrived)
        .reshape(mode_count, space_dims, cell_rows, cell_cols)
    )
    rim_width = SWEEPS + 1
    source_padded = padded_2(deposit, (("slab", 2), ("cross", 3)), rim_width)
    grid_x = (
        lax.axis_index("slab") * cell_rows
        - rim_width
        + jnp.arange(cell_rows + 2 * rim_width, dtype=jnp.int32)
    )
    grid_y = (
        lax.axis_index("cross") * cell_cols
        - rim_width
        + jnp.arange(cell_cols + 2 * rim_width, dtype=jnp.int32)
    )
    inside_x = (grid_x >= 0) & (grid_x < cell_rows * slab_count)
    inside_y = (grid_y >= 0) & (grid_y < cell_cols * cross_count)
    inside_mask = (inside_x[:, None] & inside_y[None, :]).astype(jnp.float32)
    field_now = source_padded
    for sweep_index in range(SWEEPS):
        edge_start = sweep_index + 1
        upper_x = cell_rows + 2 * rim_width - edge_start
        upper_y = cell_cols + 2 * rim_width - edge_start
        neighbours = (
            field_now[..., 2:, 1:-1]
            + field_now[..., :-2, 1:-1]
            + field_now[..., 1:-1, 2:]
            + field_now[..., 1:-1, :-2]
        )
        field_now = (
            source_padded[..., edge_start:upper_x, edge_start:upper_y] + SPREAD * neighbours
        ) * inside_mask[edge_start:upper_x, edge_start:upper_y]
    lift_padded = padded_2(lift_matrix, (("slab", 2), ("cross", 3)), 1)
    state_padded = lift_state(lift_padded.astype(jnp.float32), field_now)
    blocks = offset_blocks(neighbour_codes, jacobian)
    induced = apply_blocks(blocks, state_padded, cell_rows, cell_cols)
    partial_value = jnp.dot(
        induced.reshape(mode_count, -1),
        pod_basis.reshape(-1, pod_basis.shape[-1]),
        precision=lax.Precision.HIGHEST,
        preferred_element_type=jnp.float32,
    )
    reduced = lax.psum(partial_value, ("slab", "cross"))
    return (induced, reduced)


def solution(mesh):
    in_specs = (
        P(None, None, ("slab", "cross")),
        P(None, ("slab", "cross")),
        P(None, ("slab", "cross")),
        P(("slab", "cross"), None),
        P(("slab", "cross")),
        P(None, "slab", "cross"),
        P("groups", None, None, "slab", "cross"),
        P("groups", None, "slab", "cross"),
        P("groups", "slab", "cross", None),
    )
    out_specs = (P("groups", None, "slab", "cross"), P("groups", None))
    slabs, crosses = mesh.shape["slab"], mesh.shape["cross"]
    chosen = fast_body if crosses == 2 and slabs == 8 else body
    return jax.shard_map(chosen, mesh=mesh, in_specs=in_specs, out_specs=out_specs, check_vma=False)
```

```python
import functools

import jax
import jax.numpy as jnp
from jax import lax
from jax.experimental import pallas as pl
from jax.experimental.pallas import tpu as pltpu
from jax.sharding import PartitionSpec as P

SWEEPS = 4


SPREAD = 0.24

RIM = SWEEPS + 1

LANES = 128

MESH = pl.DeviceIdType.MESH

NT = (((1,), (1,)), ((), ()))


def split_2(value):
    high = value.astype(jnp.bfloat16)
    low = (value - high.astype(jnp.float32)).astype(jnp.bfloat16)
    return high, low


def whole_kernel(
    slabs,
    rows,
    modes_dim,
    comps,
    variables,
    node_total,
    shapes_hbm,
    stencil_hbm,
    weight_hbm,
    owner_hbm,
    target_hbm,
    lift_hbm,
    codes_hbm,
    jac_hbm,
    pod_hbm,
    induced_ref,
    reduced_ref,
    stencil_ref,
    weight_ref,
    owner_ref,
    target_ref,
    lift_ref,
    codes_ref,
    jac_ref,
    pod_ref,
    modes_ref,
    field_ref,
    scale_ref,
    send_buf,
    recv_buf,
    arrived,
    labels,
    squares,
    field_1,
    field_2,
    field_3,
    field_4,
    state,
    blocks,
    pending,
    part_ref,
    pair_part,
    chip_sum,
    got,
    sum_ref,
    fetch_sem,
    send_sem,
    recv_sem,
    edge_send,
    edge_recv,
    pair_send,
    pair_recv,
    sq_send,
    sq_recv,
    part_send,
    part_recv,
    back_send,
    back_recv,
):
    me = lax.axis_index("slab")
    mine = lax.axis_index("cross")
    other = 1 - mine
    nodes = modes_ref.shape[1]
    data = modes_dim * comps
    surf = stencil_ref.shape[1]

    fetched = [
        pltpu.make_async_copy(source, held, fetch_sem.at[n])
        for n, (source, held) in enumerate(
            (
                (shapes_hbm, modes_ref.at[pl.ds(0, data)]),
                (stencil_hbm, stencil_ref),
                (weight_hbm, weight_ref),
                (owner_hbm, owner_ref),
                (target_hbm, target_ref),
                (lift_hbm, lift_ref),
                (codes_hbm, codes_ref),
                (jac_hbm, jac_ref),
                (pod_hbm, pod_ref),
            )
        )
    ]
    for copy in fetched:
        copy.start()

    barrier = pltpu.get_barrier_semaphore()
    for k in range(1, slabs):
        pl.semaphore_signal(
            barrier, inc=1, device_id={"slab": lax.rem(me + k, slabs)}, device_id_type=MESH
        )
    pl.semaphore_signal(barrier, inc=1, device_id={"cross": other}, device_id_type=MESH)

    for copy in fetched[0:6]:
        copy.wait()
    modes_ref[data:, :] = jnp.zeros((LANES - data, nodes), jnp.float32)

    node_id = lax.broadcasted_iota(jnp.int32, (nodes, surf), 0)
    mix = jnp.zeros((nodes, surf), jnp.float32)
    for j in range(stencil_ref.shape[0]):
        mix = mix + jnp.where(stencil_ref[j : j + 1, :] == node_id, weight_ref[j : j + 1, :], 0.0)
    surface = jnp.dot(
        modes_ref[...], mix, precision=lax.Precision.HIGHEST, preferred_element_type=jnp.float32
    )
    owner = owner_ref[...]
    slab_id = lax.broadcasted_iota(jnp.int32, (slabs, surf), 0)
    named = (owner == slab_id).astype(jnp.float32)
    before = (
        lax.broadcasted_iota(jnp.int32, (surf, surf), 0)
        < lax.broadcasted_iota(jnp.int32, (surf, surf), 1)
    ).astype(jnp.bfloat16)
    ahead = jnp.dot(named.astype(jnp.bfloat16), before, preferred_element_type=jnp.float32)
    rank = jnp.sum(ahead * named, axis=0, keepdims=True).astype(jnp.int32)
    position = owner * LANES + rank
    target = target_ref[...]
    target_low = lax.rem(target, 64)
    row_id = lax.broadcasted_iota(jnp.int32, surface.shape, 0)
    high = surface.astype(jnp.bfloat16).astype(jnp.float32)
    low = surface - high
    high = jnp.where(row_id == data, (target - target_low).astype(jnp.float32), high)
    high = jnp.where(row_id == data + 1, 1.0, high)
    low = jnp.where(row_id == data, target_low.astype(jnp.float32), low)
    both = jnp.concatenate([high, low], axis=0).astype(jnp.bfloat16)
    modes = modes_ref[...]
    square_row = lax.dot_general(
        jnp.ones((8, nodes), jnp.float32),
        modes * modes,
        NT,
        precision=lax.Precision.HIGHEST,
        preferred_element_type=jnp.float32,
    )[0:1]
    slot_id = lax.broadcasted_iota(jnp.int32, (LANES, surf), 0)
    out_rows = send_buf.shape[1]
    out_id = lax.broadcasted_iota(jnp.int32, (out_rows, LANES), 0)

    pl.semaphore_wait(barrier, slabs)
    copies = []
    for step in range(slabs):
        k = (step + 1) % slabs
        dest = lax.rem(me + k, slabs)
        onehot = (position == slot_id + dest * LANES).astype(jnp.float32).astype(jnp.bfloat16)
        packed = lax.dot_general(both, onehot, NT, preferred_element_type=jnp.float32)
        block = packed[0:out_rows] + packed[LANES : LANES + out_rows]
        empty = 1.0 - block[data + 1 : data + 2]
        block = jnp.where(out_id == data, block - 65536.0 * empty, block)
        block = jnp.where(out_id == data + 2, square_row, block)
        if k == 0:
            recv_buf[0] = block
        else:
            send_buf[k] = block
            copy = pltpu.make_async_remote_copy(
                src_ref=send_buf.at[k],
                dst_ref=recv_buf.at[k],
                send_sem=send_sem.at[k],
                recv_sem=recv_sem.at[k],
                device_id={"slab": dest},
                device_id_type=MESH,
            )
            copy.start()
            copies.append(copy)

    for comp in range(comps):
        for b in range(variables):
            field_ref[mine, RIM : RIM + rows, data + comp * variables + b, :] = lift_ref[
                b, comp
            ].astype(jnp.float32)
    field_ref[mine, RIM : RIM + rows, data + comps * variables, :] = jnp.zeros(
        (rows, LANES), jnp.float32
    )

    @pl.when(me == 0)
    def _():
        field_ref[mine, 0:RIM] = jnp.zeros((RIM,) + field_ref.shape[2:], jnp.float32)

    @pl.when(me == slabs - 1)
    def _():
        field_ref[mine, RIM + rows :] = jnp.zeros((RIM,) + field_ref.shape[2:], jnp.float32)

    for copy in fetched[6:8]:
        copy.wait()
    square = variables * variables

    def select(pair, carry):
        for x0 in range(0, rows, 8):
            chosen = [jac_ref[k, pair, x0 : x0 + 8, :].astype(jnp.float32) for k in range(7)]
            codes = [codes_ref[k, x0 : x0 + 8, :] for k in range(7)]
            for code in range(9):
                value = jnp.zeros((8, LANES), jnp.float32)
                for k in range(7):
                    value = jnp.where(codes[k] == code, chosen[k], value)
                blocks[code * square + pair, x0 : x0 + 8, :] = value
        return carry

    lax.fori_loop(0, square, select, 0)

    total = square_row
    for k in range(slabs):
        if k > 0:
            copies[k - 1].wait_recv()
            total = total + recv_buf[k, data + 2 : data + 3]
        head, tail = split_2(recv_buf[k, 0:data])
        arrived[0:data, k * LANES : (k + 1) * LANES] = head
        arrived[data:, k * LANES : (k + 1) * LANES] = tail
        labels[0:1, k * LANES : (k + 1) * LANES] = recv_buf[k, data : data + 1].astype(jnp.int32)

    squares[0] = jnp.broadcast_to(total, (8, LANES))
    sq_copy = pltpu.make_async_remote_copy(
        src_ref=squares.at[0],
        dst_ref=squares.at[1],
        send_sem=sq_send,
        recv_sem=sq_recv,
        device_id={"cross": other},
        device_id_type=MESH,
    )
    sq_copy.start()

    cell_id = lax.broadcasted_iota(jnp.int32, (2 * LANES, slabs * LANES), 0)
    pairs = rows // 2

    def deposit(i, carry):
        pair = lax.rem(i + pairs - 3, pairs)
        hit = (labels[0:1, :] == cell_id + pair * (2 * LANES)).astype(jnp.float32)
        got = lax.dot_general(
            arrived[...], hit.astype(jnp.bfloat16), NT, preferred_element_type=jnp.float32
        )
        got = got[0:data] + got[data:]
        field_ref[mine, RIM + 2 * pair, 0:data, :] = got[:, 0:LANES]
        field_ref[mine, RIM + 2 * pair + 1, 0:data, :] = got[:, LANES:]
        return carry

    up = pltpu.make_async_remote_copy(
        src_ref=field_ref.at[mine, pl.ds(rows, RIM)],
        dst_ref=field_ref.at[mine, pl.ds(0, RIM)],
        send_sem=edge_send.at[0],
        recv_sem=edge_recv.at[0],
        device_id={"slab": lax.rem(me + 1, slabs)},
        device_id_type=MESH,
    )
    down = pltpu.make_async_remote_copy(
        src_ref=field_ref.at[mine, pl.ds(RIM, RIM)],
        dst_ref=field_ref.at[mine, pl.ds(RIM + rows, RIM)],
        send_sem=edge_send.at[1],
        recv_sem=edge_recv.at[1],
        device_id={"slab": lax.rem(me + slabs - 1, slabs)},
        device_id_type=MESH,
    )

    def across(n, start, size):
        return pltpu.make_async_remote_copy(
            src_ref=field_ref.at[mine, pl.ds(start, size)],
            dst_ref=field_ref.at[mine, pl.ds(start, size)],
            send_sem=pair_send.at[n],
            recv_sem=pair_recv.at[n],
            device_id={"cross": other},
            device_id_type=MESH,
        )

    third = (pairs - 6) // 2
    middle = [
        across(0, RIM + rows - 6, 6),
        across(1, RIM, 6),
        across(2, RIM + 6, 2 * third),
        across(3, RIM + 6 + 2 * third, rows - 12 - 2 * third),
    ]
    low_rim = across(4, 0, RIM)
    high_rim = across(5, RIM + rows, RIM)

    lax.fori_loop(0, 3, deposit, 0)

    @pl.when(me < slabs - 1)
    def _():
        up.start()

    middle[0].start()
    lax.fori_loop(3, 6, deposit, 0)

    @pl.when(me > 0)
    def _():
        down.start()

    middle[1].start()
    lax.fori_loop(6, 6 + third, deposit, 0)
    middle[2].start()
    lax.fori_loop(6 + third, pairs, deposit, 0)
    middle[3].start()

    sq_copy.wait()
    whole = squares[0, 0:1] + squares[1, 0:1]
    lane = lax.broadcasted_iota(jnp.int32, (modes_dim, LANES), 1)
    mode = lax.broadcasted_iota(jnp.int32, (modes_dim, LANES), 0)
    per_mode = jnp.sum(
        jnp.where((lax.rem(lane, modes_dim) == mode) & (lane < data), whole, 0.0),
        axis=1,
        keepdims=True,
    )
    inverse = 1.0 / jnp.sqrt(per_mode / node_total + 1e-06)
    scale_ref[...] = jnp.broadcast_to(inverse, scale_ref.shape)

    planes = rows + 2 * RIM
    lane = lax.broadcasted_iota(jnp.int32, (modes_dim, LANES), 1)
    first, last = lane == 0, lane == LANES - 1

    def sweep(source, result, x, inside):
        for comp in range(comps):
            part = pl.ds(comp * modes_dim, modes_dim)
            left, right = source[0, x, part, :], source[1, x, part, :]
            near_left = pltpu.roll(jnp.where(last, 0.0, left), 1, 1) + pltpu.roll(
                jnp.where(first, right, left), LANES - 1, 1
            )
            near_right = pltpu.roll(jnp.where(last, left, right), 1, 1) + pltpu.roll(
                jnp.where(first, 0.0, right), LANES - 1, 1
            )
            for tile, near in ((0, near_left), (1, near_right)):
                near = near + source[tile, x - 1, part, :] + source[tile, x + 1, part, :]
                value = field_ref[tile, x, part, :] + SPREAD * near
                result[tile, x, part, :] = value if inside is None else value * inside

    fields = [field_1, field_2, field_3, field_4]
    stages = [field_ref, *fields]

    def inner(step):
        def plane(x, carry):
            sweep(stages[step - 1], stages[step], x, None)
            return carry

        count = rows - 2 * step
        lax.fori_loop(
            RIM + step, RIM + rows - step, plane, 0, unroll=4 if count % 4 == 0 else 2
        )

    def outer(step):
        def plane(i, carry):
            for x in (step + i, planes - RIM - step + i):
                at = x - RIM + me * rows
                inside = ((at >= 0) & (at < slabs * rows)).astype(jnp.float32)
                sweep(stages[step - 1], stages[step], x, inside)
            return carry

        lax.fori_loop(0, RIM, plane, 0, unroll=5)

    for copy in middle:
        copy.wait_recv()
    for step in range(1, SWEEPS):
        inner(step)

    @pl.when(me > 0)
    def _():
        up.wait_recv()

    low_rim.start()

    @pl.when(me < slabs - 1)
    def _():
        down.wait_recv()

    high_rim.start()
    inner(SWEEPS)
    low_rim.wait_recv()
    high_rim.wait_recv()
    for step in range(1, SWEEPS + 1):
        outer(step)
    pong = fields[SWEEPS - 1]

    here = (mine == 0).astype(jnp.float32)
    there = 1.0 - here

    def lift(x, carry):
        for b in range(variables):
            own = jnp.zeros((modes_dim, LANES), jnp.float32)
            far = jnp.zeros((modes_dim, LANES), jnp.float32)
            for comp in range(comps):
                part = pl.ds(comp * modes_dim, modes_dim)
                row = pl.ds(data + comp * variables + b, 1)
                own = own + field_ref[mine, x + RIM - 1, row, :] * pong[mine, x + RIM - 1, part, :]
                far = (
                    far + field_ref[other, x + RIM - 1, row, :] * pong[other, x + RIM - 1, part, :]
                )
            state[1, x, b] = own
            state[0, x, b] = pltpu.roll(jnp.where(last, far * there, own), 1, 1)
            state[2, x, b] = pltpu.roll(jnp.where(first, far * here, own), LANES - 1, 1)
        return carry

    lax.fori_loop(0, rows + 2, lift, 0, unroll=2)

    stride = variables * rows

    def project(x, total):
        for b in range(variables):
            total = total + jnp.dot(
                pending[:, b * LANES : (b + 1) * LANES],
                pod_ref[b, x],
                preferred_element_type=jnp.float32,
            )
        return total

    def apply(x, total):
        total = project(jnp.maximum(x - 1, 0), total)
        sums = [jnp.zeros((modes_dim, LANES), jnp.float32) for _ in range(variables)]
        for code in range(9):
            for a in range(variables):
                value = state[code % 3, x + code // 3, a]
                for b in range(variables):
                    gain = blocks[code * square + b * variables + a, pl.ds(x, 1), :]
                    sums[b] = sums[b] + gain * value
        for b in range(variables):
            result = sums[b] * scale_ref[...]
            induced_ref[pl.ds(b * rows + x, modes_dim, stride=stride), :] = result
            high, low = split_2(result)
            pending[0:modes_dim, b * LANES : (b + 1) * LANES] = high
            pending[modes_dim:, b * LANES : (b + 1) * LANES] = low
        return total

    fetched[8].wait()
    pending[...] = jnp.zeros(pending.shape, jnp.bfloat16)
    total = lax.fori_loop(
        0, rows, apply, jnp.zeros((2 * modes_dim, reduced_ref.shape[1]), jnp.float32), unroll=2
    )
    total = project(rows - 1, total)
    result = total[0:modes_dim] + total[modes_dim:]
    half = modes_dim // 2
    part_ref[0] = result[0:half]
    part_ref[1] = result[half:]
    to_pair = pltpu.make_async_remote_copy(
        src_ref=part_ref.at[other],
        dst_ref=pair_part,
        send_sem=back_send.at[0],
        recv_sem=back_recv.at[0],
        device_id={"cross": other},
        device_id_type=MESH,
    )
    to_pair.start()
    to_pair.wait()
    chip_sum[...] = part_ref[mine] + pair_part[...]
    parts = []
    for k in range(1, slabs):
        copy = pltpu.make_async_remote_copy(
            src_ref=chip_sum,
            dst_ref=got.at[me],
            send_sem=part_send.at[k],
            recv_sem=part_recv.at[k],
            device_id={"slab": lax.rem(me + k, slabs)},
            device_id_type=MESH,
        )
        copy.start()
        parts.append(copy)
    got[me] = chip_sum[...]
    for copy in parts:
        copy.wait()
    whole_sum = got[0]
    for n in range(1, slabs):
        whole_sum = whole_sum + got[n]
    sum_ref[mine] = whole_sum
    back = pltpu.make_async_remote_copy(
        src_ref=sum_ref.at[mine],
        dst_ref=sum_ref.at[mine],
        send_sem=back_send.at[1],
        recv_sem=back_recv.at[1],
        device_id={"cross": other},
        device_id_type=MESH,
    )
    back.start()
    back.wait()
    reduced_ref[0:half, :] = sum_ref[0]
    reduced_ref[half:, :] = sum_ref[1]
    for copy in middle:
        copy.wait_send()
    low_rim.wait_send()
    high_rim.wait_send()
    for copy in copies:
        copy.wait_send()

    @pl.when(me < slabs - 1)
    def _():
        up.wait_send()

    @pl.when(me > 0)
    def _():
        down.wait_send()


VMEM = pl.BlockSpec(memory_space=pltpu.VMEM)

ANY = pl.BlockSpec(memory_space=pl.ANY)


def fast_body(
    mode_shapes,
    stencil,
    stencil_weight,
    owner_slab,
    target_cell,
    neighbour_codes,
    jacobian,
    lift_matrix,
    pod_basis,
):
    slabs = lax.axis_size("slab")
    crosses = lax.axis_size("cross")
    modes_dim, comps, nodes = mode_shapes.shape
    surf = owner_slab.shape[0]
    rows, cols = neighbour_codes.shape[1:]
    variables = lift_matrix.shape[0]
    pod = pod_basis.shape[-1]
    data = modes_dim * comps
    planes = rows + 2 * RIM
    count = slabs * crosses
    half = modes_dim // 2
    dma = pltpu.SemaphoreType.DMA
    operands = (
        mode_shapes.transpose(1, 0, 2).reshape(data, nodes),
        stencil,
        stencil_weight,
        owner_slab.reshape(1, surf),
        target_cell.reshape(1, surf),
        lift_matrix,
        neighbour_codes,
        jacobian.reshape(jacobian.shape[0], variables * variables, rows, cols),
        pod_basis,
    )
    sweep_shape = pltpu.VMEM((crosses, planes, data, cols), jnp.float32)
    induced, reduced = pl.pallas_call(
        functools.partial(
            whole_kernel,
            slabs,
            rows,
            modes_dim,
            comps,
            variables,
            float(comps * nodes * count),
        ),
        out_shape=(
            jax.ShapeDtypeStruct((modes_dim * variables * rows, cols), jnp.float32),
            jax.ShapeDtypeStruct((modes_dim, pod), jnp.float32),
        ),
        in_specs=[ANY] * len(operands),
        out_specs=(VMEM, VMEM),
        scratch_shapes=[pltpu.VMEM(x.shape, x.dtype) for x in operands[1:]]
        + [
            pltpu.VMEM((LANES, nodes), jnp.float32),
            pltpu.VMEM((crosses, planes, data + 16, cols), jnp.float32),
            pltpu.VMEM((modes_dim, LANES), jnp.float32),
            pltpu.VMEM((slabs, data + 8, LANES), jnp.float32),
            pltpu.VMEM((slabs, data + 8, LANES), jnp.float32),
            pltpu.VMEM((2 * data, slabs * LANES), jnp.bfloat16),
            pltpu.VMEM((8, slabs * LANES), jnp.int32),
            pltpu.VMEM((2, 8, LANES), jnp.float32),
            sweep_shape,
            sweep_shape,
            sweep_shape,
            sweep_shape,
            pltpu.VMEM((3, rows + 2, variables, modes_dim, cols), jnp.float32),
            pltpu.VMEM((9 * variables * variables, rows, cols), jnp.float32),
            pltpu.VMEM((2 * modes_dim, variables * cols), jnp.bfloat16),
            pltpu.VMEM((2, half, pod), jnp.float32),
            pltpu.VMEM((half, pod), jnp.float32),
            pltpu.VMEM((half, pod), jnp.float32),
            pltpu.VMEM((slabs, half, pod), jnp.float32),
            pltpu.VMEM((2, half, pod), jnp.float32),
            dma((len(operands),)),
            dma((slabs,)),
            dma((slabs,)),
            dma((2,)),
            dma((2,)),
            dma((6,)),
            dma((6,)),
            dma,
            dma,
            dma((slabs,)),
            dma((slabs,)),
            dma((2,)),
            dma((2,)),
        ],
        compiler_params=pltpu.CompilerParams(
            collective_id=0, has_side_effects=True, vmem_limit_bytes=56 * 1024 * 1024
        ),
    )(*operands)
    return induced.reshape(modes_dim, variables, rows, cols), reduced


def padded_2(block, sides, width):
    for axis, dim in sides:
        count = lax.axis_size(axis)
        forward = [(i, i + 1) for i in range(count - 1)]
        backward = [(target, source) for source, target in forward]
        low = lax.ppermute(
            lax.slice_in_dim(block, block.shape[dim] - width, None, axis=dim), axis, forward
        )
        high = lax.ppermute(lax.slice_in_dim(block, 0, width, axis=dim), axis, backward)
        block = jnp.concatenate([low, block, high], axis=dim)
    return block


def lift_state(lift_gain, field_now):
    accumulated = 0.0
    for component in range(lift_gain.shape[1]):
        accumulated = accumulated + lift_gain[:, component] * jnp.expand_dims(
            field_now[..., component, :, :], -3
        )
    return accumulated


def offset_blocks(codes, jacobian):
    zero_block = jnp.zeros((), jnp.bfloat16)
    stacked = []
    for offset_code in range(9):
        chosen = jnp.where((codes == offset_code)[:, None, None], jacobian, zero_block)
        stacked.append(jnp.sum(chosen, axis=0, dtype=jnp.float32))
    return jnp.stack(stacked)


def apply_blocks(blocks, padded, cell_rows, cell_cols):
    accumulated = 0.0
    for offset_code in range(9):
        start_x = offset_code // 3
        start_y = offset_code % 3
        shifted = padded[..., start_x : start_x + cell_rows, start_y : start_y + cell_cols]
        for component in range(blocks.shape[2]):
            accumulated = accumulated + blocks[offset_code, :, component] * jnp.expand_dims(
                shifted[..., component, :, :], -3
            )
    return accumulated


def body(
    mode_shapes,
    stencil,
    stencil_weight,
    owner_slab,
    target_cell,
    neighbour_codes,
    jacobian,
    lift_matrix,
    pod_basis,
):
    slab_count = lax.axis_size("slab")
    cross_count = lax.axis_size("cross")
    mode_count, space_dims, nodes_dev = mode_shapes.shape
    surf_dev = owner_slab.shape[0]
    capacity = 2 * surf_dev // slab_count
    cell_rows = neighbour_codes.shape[1]
    cell_cols = neighbour_codes.shape[2]
    total_nodes = nodes_dev * slab_count * cross_count
    squares = jnp.sum(mode_shapes * mode_shapes, axis=(1, 2))
    scale_rms = jnp.sqrt(lax.psum(squares, ("slab", "cross")) / (space_dims * total_nodes) + 1e-06)
    shapes_used = mode_shapes / scale_rms[:, None, None]
    picked = shapes_used[:, :, stencil]
    surface = jnp.sum(stencil_weight[None, None] * picked, axis=2)
    dest_slab = owner_slab[:, 0]
    onehot = (dest_slab[:, None] == jnp.arange(slab_count, dtype=jnp.int32)[None, :]).astype(
        jnp.int32
    )
    slot_rank = jnp.sum((jnp.cumsum(onehot, axis=0) - 1) * onehot, axis=1)
    position = dest_slab * capacity + slot_rank
    payload = jnp.zeros((mode_count * space_dims, slab_count * capacity), jnp.float32)
    payload = payload.at[:, position].set(surface.reshape(mode_count * space_dims, surf_dev))
    labels = jnp.zeros((1, slab_count * capacity), jnp.int32).at[0, position].set(target_cell)
    arrived, arrived_cells = (
        lax.all_to_all(payload, "slab", split_axis=1, concat_axis=1, tiled=True),
        lax.all_to_all(labels, "slab", split_axis=1, concat_axis=1, tiled=True),
    )
    deposit = jnp.zeros((mode_count * space_dims, cell_rows * cell_cols), jnp.float32)
    deposit = (
        deposit.at[:, arrived_cells[0]]
        .add(arrived)
        .reshape(mode_count, space_dims, cell_rows, cell_cols)
    )
    rim_width = SWEEPS + 1
    source_padded = padded_2(deposit, (("slab", 2), ("cross", 3)), rim_width)
    grid_x = (
        lax.axis_index("slab") * cell_rows
        - rim_width
        + jnp.arange(cell_rows + 2 * rim_width, dtype=jnp.int32)
    )
    grid_y = (
        lax.axis_index("cross") * cell_cols
        - rim_width
        + jnp.arange(cell_cols + 2 * rim_width, dtype=jnp.int32)
    )
    inside_x = (grid_x >= 0) & (grid_x < cell_rows * slab_count)
    inside_y = (grid_y >= 0) & (grid_y < cell_cols * cross_count)
    inside_mask = (inside_x[:, None] & inside_y[None, :]).astype(jnp.float32)
    field_now = source_padded
    for sweep_index in range(SWEEPS):
        edge_start = sweep_index + 1
        upper_x = cell_rows + 2 * rim_width - edge_start
        upper_y = cell_cols + 2 * rim_width - edge_start
        neighbours = (
            field_now[..., 2:, 1:-1]
            + field_now[..., :-2, 1:-1]
            + field_now[..., 1:-1, 2:]
            + field_now[..., 1:-1, :-2]
        )
        field_now = (
            source_padded[..., edge_start:upper_x, edge_start:upper_y] + SPREAD * neighbours
        ) * inside_mask[edge_start:upper_x, edge_start:upper_y]
    lift_padded = padded_2(lift_matrix, (("slab", 2), ("cross", 3)), 1)
    state_padded = lift_state(lift_padded.astype(jnp.float32), field_now)
    blocks = offset_blocks(neighbour_codes, jacobian)
    induced = apply_blocks(blocks, state_padded, cell_rows, cell_cols)
    partial_value = jnp.dot(
        induced.reshape(mode_count, -1),
        pod_basis.reshape(-1, pod_basis.shape[-1]),
        precision=lax.Precision.HIGHEST,
        preferred_element_type=jnp.float32,
    )
    reduced = lax.psum(partial_value, ("slab", "cross"))
    return (induced, reduced)


def solution(mesh):
    in_specs = (
        P(None, None, ("slab", "cross")),
        P(None, ("slab", "cross")),
        P(None, ("slab", "cross")),
        P(("slab", "cross"), None),
        P(("slab", "cross")),
        P(None, "slab", "cross"),
        P("groups", None, None, "slab", "cross"),
        P("groups", None, "slab", "cross"),
        P("groups", "slab", "cross", None),
    )
    out_specs = (P("groups", None, "slab", "cross"), P("groups", None))
    slabs, crosses = mesh.shape["slab"], mesh.shape["cross"]
    chosen = fast_body if crosses == 2 and slabs == 8 else body
    return jax.shard_map(chosen, mesh=mesh, in_specs=in_specs, out_specs=out_specs, check_vma=False)
```
